512 devices in a mesh: gx: 64 (over x, y, core), gy: 8 (over z).
Axes of the slice: x: 4, y: 8, z: 8, core: 2. Of those that a mesh axis runs over, the one named last changes fastest.
Arguments:
- cells: int32 [3, 64, 8, 4, 256], P(None, 'gx', 'gy'), may hold values from 1 to 509, as said below
- offsets: float32 [3, 64, 8, 4, 256], P(None, 'gx', 'gy'), may hold values from 0 to 1
- counts: int32 [64, 8, 4], P('gx', 'gy'), may hold values from 16 to 256, as said below
- observed: float32 [64, 8, 4, 256], P('gx', 'gy'), may hold values from -12 to 12
- noise: float32 [64, 8, 4, 256], P('gx', 'gy'), may hold values from 0.1 to 1
- kernel_x: bfloat16 [256, 256], replicated, may hold values from -2 to 2, as said below
- kernel_y: bfloat16 [512, 512], replicated, may hold values from -2 to 2, as said below
- kernel_t: bfloat16 [128, 128], replicated, may hold values from -2 to 2, as said below
Outputs:
- solution: float32 [64, 8, 4, 256], P('gx', 'gy')
- residual: float32 [64, 8, 4, 256], P('gx', 'gy')
The draws below stay inside these ranges and needn't reach their ends.
Inputs may be any that keep to these rules, and one draw needn't show every extreme that they name: cells[0], cells[1], cells[2] are a slot's x, y and t cell. Slot (bx, by, k, s) has 4 bx <= x < 4 bx + 4 and 64 by + 16 k <= y < 64 by + 16 k + 16; each coordinate lies from 1 to its grid size minus 3. Only the first counts[bx, by, k] slots of tile (bx, by, k) are live; some tile is full. kernel_x is symmetric and positive definite. kernel_y is symmetric and positive definite. kernel_t is symmetric and positive definite.
All inputs are finite; a program needn't handle non-finite values.
Results may differ from the reference program's by a relative error of at most 0.04.
Values may be sent and summed in bfloat16 or wider, within the bound.
A program may use at most 64 MiB of HBM per device.

```python
import math
import jax
import jax.numpy as jnp
from jax import lax

XS = 4
YS = 64
NT = 128
TY = 16
CAP = 256
ITERS = 2
NBX = 64
NBY = 8
TILES = 4
NX = 256
NY = 512


def covariance(key, order):
    integers = jax.random.randint(key, (order, order), -2, 3).astype(jnp.float32)
    gram = jnp.dot(integers, integers.T, precision=lax.Precision.HIGHEST)
    identity = (lax.broadcasted_iota(jnp.int32, (order, order), 0) == lax.broadcasted_iota(jnp.int32, (order, order), 1)).astype(jnp.float32)
    return ((gram + 0.25 * order * identity) / (2.25 * order)).astype(jnp.bfloat16)


def draw_kernel_x(key, part):
    key = jax.random.fold_in(key, 11)
    return covariance(key, NX)


def draw_kernel_y(key, part):
    key = jax.random.fold_in(key, 13)
    return covariance(key, NY)


def draw_kernel_t(key, part):
    key = jax.random.fold_in(key, 17)
    return covariance(key, NT)


def draw_cells(key, part):
    key = jax.random.fold_in(key, 3)
    key_x, key_y, key_t = jax.random.split(key, 3)
    shape_slots = (NBX, NBY, TILES, CAP)
    along_x = XS * lax.broadcasted_iota(jnp.int32, shape_slots, 0) + jax.random.randint(key_x, shape_slots, 0, XS)
    along_y = YS * lax.broadcasted_iota(jnp.int32, shape_slots, 1) + TY * lax.broadcasted_iota(jnp.int32, shape_slots, 2) + jax.random.randint(key_y, shape_slots, 0, TY)
    along_t = jax.random.randint(key_t, shape_slots, 0, NT)
    return jnp.stack([jnp.clip(along_x, 1, NX - 3), jnp.clip(along_y, 1, NY - 3), jnp.clip(along_t, 1, NT - 3)])


def draw_counts(key, part):
    key = jax.random.fold_in(key, 7)
    key_level, key_base, key_cx, key_cy, key_ct = jax.random.split(key, 5)
    shape_tiles = (NBX, NBY, TILES)
    level = jnp.left_shift(jnp.int32(1), jax.random.randint(key_level, (NBX, NBY, 1), 0, 3))
    base = jax.random.randint(key_base, shape_tiles, CAP // 4, CAP + 1)
    rising = NBX + 2 * lax.broadcasted_iota(jnp.int32, shape_tiles, 0)
    filled = jnp.minimum(CAP, base * level * rising // (4 * NBX))
    chosen_x = jax.random.randint(key_cx, (), 0, NBX)
    chosen_y = jax.random.randint(key_cy, (), 0, NBY)
    chosen_t = jax.random.randint(key_ct, (), 0, TILES)
    full_tile = (lax.broadcasted_iota(jnp.int32, shape_tiles, 0) == chosen_x) & (lax.broadcasted_iota(jnp.int32, shape_tiles, 1) == chosen_y) & (lax.broadcasted_iota(jnp.int32, shape_tiles, 2) == chosen_t)
    return jnp.where(full_tile, CAP, filled)


def draw_observed(key, part):
    key = jax.random.fold_in(key, 5)
    key_scale, key_value = jax.random.split(key)
    scales = jnp.exp(jax.random.uniform(key_scale, (NBX, NBY, TILES, 1), jnp.float32, math.log(0.3), math.log(3.0)))
    values = jnp.clip(jax.random.normal(key_value, (NBX, NBY, TILES, CAP), jnp.float32), -4.0, 4.0)
    return values * scales


def levels(stream_key, shape, cuts, least, high):
    def one(position, parts):
        draws = jax.random.uniform(jax.random.fold_in(jax.random.fold_in(stream_key, 6), position), (parts,), jnp.float32, least / len(cuts), high / len(cuts))
        return jnp.repeat(jnp.exp(draws), shape[position] // parts).reshape((-1,) + (1,) * (len(shape) - position - 1))

    gain = one(*cuts[0])
    for cut in cuts[1:]:
        gain = gain * one(*cut)
    return gain


def setup_inputs(seed: int = 0) -> dict:
    key_list = jax.random.split(jax.random.key(seed), 9)
    cells = draw_cells(jax.random.fold_in(key_list[8], 71), 0)
    offsets = jnp.clip(1.0 * jax.random.uniform(key_list[1], (3, NBX, NBY, TILES, CAP), jnp.float32) ** levels(key_list[1], (3, NBX, NBY, TILES, CAP), ((1, 64), (2, 8)), -0.2, 0.2), 0.0, 1.0)
    counts = draw_counts(jax.random.fold_in(key_list[8], 71), 0)
    observed = draw_observed(jax.random.fold_in(key_list[8], 71), 0)
    noise = jnp.clip(jnp.exp(math.log(1.0) - 2.3025851 * jax.random.uniform(key_list[4], (NBX, NBY, TILES, CAP), jnp.float32) ** levels(key_list[4], (NBX, NBY, TILES, CAP), ((0, 64), (1, 8)), -0.2, 0.2)), 0.1, 1.0)
    kernel_x = draw_kernel_x(jax.random.fold_in(key_list[8], 71), 0)
    kernel_y = draw_kernel_y(jax.random.fold_in(key_list[8], 71), 0)
    kernel_t = draw_kernel_t(jax.random.fold_in(key_list[8], 71), 0)
    return dict(cells=cells, offsets=offsets, counts=counts, observed=observed, noise=noise, kernel_x=kernel_x, kernel_y=kernel_y, kernel_t=kernel_t)


def cubic_weights(fraction):
    square = fraction * fraction
    cubic_term = square * fraction
    return jnp.stack([(2.0 * square - cubic_term - fraction) * 0.5, (3.0 * cubic_term - 5.0 * square + 2.0) * 0.5, (4.0 * square - 3.0 * cubic_term + fraction) * 0.5, (cubic_term - square) * 0.5])


def fold_blocks(pieces, block_axis, below_width, above_width):
    number = pieces.shape[block_axis]
    span_width = pieces.shape[block_axis + 1]
    length = span_width - below_width - above_width
    middle = lax.slice_in_dim(pieces, below_width, below_width + length, axis=block_axis + 1).astype(jnp.float32)
    below_rows = lax.slice_in_dim(pieces, 0, below_width, axis=block_axis + 1).astype(jnp.float32)
    above_rows = lax.slice_in_dim(pieces, below_width + length, span_width, axis=block_axis + 1).astype(jnp.float32)
    below_zero = jnp.zeros_like(lax.slice_in_dim(below_rows, 0, 1, axis=block_axis))
    above_zero = jnp.zeros_like(lax.slice_in_dim(above_rows, 0, 1, axis=block_axis))
    below_next = jnp.concatenate([lax.slice_in_dim(below_rows, 1, number, axis=block_axis), below_zero], axis=block_axis)
    above_prev = jnp.concatenate([above_zero, lax.slice_in_dim(above_rows, 0, number - 1, axis=block_axis)], axis=block_axis)
    low_pad = [(0, 0)] * pieces.ndim
    low_pad[block_axis + 1] = (length - below_width, 0)
    high_pad = [(0, 0)] * pieces.ndim
    high_pad[block_axis + 1] = (0, length - above_width)
    summed = middle + jnp.pad(below_next, low_pad) + jnp.pad(above_prev, high_pad)
    new_shape = pieces.shape[:block_axis] + (number * length,) + pieces.shape[block_axis + 2:]
    return summed.reshape(new_shape)


def reference(cells, offsets, counts, observed, noise, kernel_x, kernel_y, kernel_t):
    wide_x = XS + 3
    wide_y = YS + 3
    slab_size = wide_x * NT * wide_y
    shape_slots = (NBX, NBY, TILES, CAP)
    live_mask = (lax.broadcasted_iota(jnp.int32, shape_slots, 3) < counts[:, :, :, None]).astype(jnp.float32)
    weight_x = cubic_weights(offsets[0])
    weight_y = cubic_weights(offsets[1])
    weight_t = cubic_weights(offsets[2])
    row_index = lax.broadcasted_iota(jnp.int32, (NBY, TILES, CAP), 0)
    kernel_t_wide = kernel_t.astype(jnp.float32)
    kernel_y_wide = kernel_y.astype(jnp.float32)

    def spread_block(inputs):
        index_x, cells_block, wx_block, wy_block, wt_block, vector_block = inputs
        local_x = cells_block[0] - XS * index_x + 1
        local_y = cells_block[1] - YS * row_index + 1
        summed = jnp.zeros((NBY * slab_size,), jnp.float32)
        for shift_x in range(4):
            for shift_y in range(4):
                for shift_t in range(4):
                    target = row_index * slab_size + ((local_x + shift_x - 1) * NT + cells_block[2] + shift_t - 1) * wide_y + local_y + shift_y - 1
                    contrib = wx_block[shift_x] * wy_block[shift_y] * wt_block[shift_t] * vector_block
                    summed = summed.at[target.reshape(-1)].add(contrib.reshape(-1))
        spread = summed.reshape(NBY, wide_x, NT, wide_y).astype(jnp.bfloat16)
        timewise = jnp.einsum("st,baty->basy", kernel_t_wide, spread.astype(jnp.float32)).astype(jnp.bfloat16)
        y_stacked = fold_blocks(jnp.moveaxis(timewise, 0, 2), 2, 1, 2).astype(jnp.bfloat16)
        return jnp.einsum("zy,aty->atz", kernel_y_wide, y_stacked.astype(jnp.float32)).astype(jnp.bfloat16)

    def apply_operator(vector):
        masked = live_mask * vector
        inputs = (jnp.arange(NBX, dtype=jnp.int32), jnp.moveaxis(cells, 1, 0), jnp.moveaxis(weight_x, 1, 0), jnp.moveaxis(weight_y, 1, 0), jnp.moveaxis(weight_t, 1, 0), masked)
        y_mixed = lax.map(spread_block, inputs)

        def mix_x(time_index):
            sheet = lax.dynamic_index_in_dim(y_mixed, time_index, axis=2, keepdims=False)
            x_stacked = fold_blocks(sheet, 0, 1, 2).astype(jnp.bfloat16)
            return jnp.dot(kernel_x, x_stacked, preferred_element_type=jnp.float32).astype(jnp.bfloat16)

        grid_field = lax.map(mix_x, jnp.arange(NT, dtype=jnp.int32))
        field_flat = grid_field.reshape(-1)
        interpolated = jnp.zeros(shape_slots, jnp.float32)
        for shift_x in range(4):
            for shift_y in range(4):
                for shift_t in range(4):
                    target = ((cells[2] + shift_t - 1) * NX + cells[0] + shift_x - 1) * NY + cells[1] + shift_y - 1
                    picked = jnp.take(field_flat, target).astype(jnp.float32)
                    interpolated = interpolated + weight_x[shift_x] * weight_y[shift_y] * weight_t[shift_t] * picked
        return live_mask * (interpolated + noise * masked)

    residual = live_mask * observed
    solution = jnp.zeros_like(residual)
    direction = residual
    norm_now = jnp.sum(residual * residual)
    for iteration in range(ITERS):
        applied = apply_operator(direction)
        step_size = norm_now / jnp.sum(direction * applied)
        solution = solution + step_size * direction
        residual = residual - step_size * applied
        if iteration + 1 < ITERS:
            norm_next = jnp.sum(residual * residual)
            direction = residual + (norm_next / norm_now) * direction
            norm_now = norm_next
    return solution, residual
```

```python
import jax
import jax.numpy as jnp
from jax import lax
from jax.experimental import pallas as pl
from jax.experimental.pallas import tpu as pltpu
from jax.sharding import PartitionSpec as P

XS = 4
YS = 64
ITERS = 2
TILES = 4
CAP = 256
SLOTS = TILES * CAP
CHIPS = 32
GROUP = 16
NX = 256
NY = 512
NT = 128
F32 = jnp.float32
BF16 = jnp.bfloat16
MESH = pl.DeviceIdType.MESH
ROW_ROW = (((1,), (1,)), ((), ()))


def cubic_weights(fraction):
    square = fraction * fraction
    cubic_term = square * fraction
    return (
        (2.0 * square - cubic_term - fraction) * 0.5,
        (3.0 * cubic_term - 5.0 * square + 2.0) * 0.5,
        (4.0 * square - 3.0 * cubic_term + fraction) * 0.5,
        (cubic_term - square) * 0.5,
    )


def iota(shape, axis):
    return lax.broadcasted_iota(jnp.int32, shape, axis)


def flat(rows):
    return jnp.concatenate([rows[k : k + 1, :] for k in range(TILES)], axis=1)


def dot(left, right):
    return jnp.dot(left, right, preferred_element_type=F32)


def dot_rows(left, right):
    return lax.dot_general(left, right, ROW_ROW, preferred_element_type=F32)


def spread_rows(weights, first, rows):
    total = jnp.zeros(rows.shape, F32)
    for shift in range(4):
        total = total + jnp.where(first + shift == rows, weights[shift], 0.0)
    return total


def third(index):
    return (index * 43) >> 7


def kernel(
    cells_ref,
    offsets_ref,
    counts_ref,
    observed_ref,
    noise_ref,
    kx_ref,
    ky_ref,
    kt_ref,
    solution_ref,
    residual_ref,
    plane,
    time_rows,
    mixed_rows,
    mix_y,
    mix_x,
    select,
    turn,
    send_a,
    recv_a,
    send_b,
    recv_b,
    send_c,
    recv_c,
    send_d,
    recv_d,
    sums,
    sums_group,
    sums_chips,
    send_sem,
    recv_sem,
    sum_send_sem,
    sum_recv_sem,
):
    block_x = lax.axis_index("gx")
    block_y = lax.axis_index("gy")
    chip = block_x // 2
    core = block_x % 2
    member = block_y * 2 + core

    def group_device(other):
        return (chip * 2 + other % 2, other // 2)

    def chip_device(other):
        return (other * 2 + core, block_y)

    barrier = pltpu.get_barrier_semaphore()

    def greet_group(step, carry):
        pl.semaphore_signal(
            barrier, inc=1, device_id=group_device((member + step) % GROUP), device_id_type=MESH
        )
        return carry

    def greet_chips(step, carry):
        pl.semaphore_signal(
            barrier, inc=1, device_id=chip_device((chip + step) % CHIPS), device_id_type=MESH
        )
        return carry

    lax.fori_loop(1, GROUP, greet_group, 0)
    lax.fori_loop(1, CHIPS, greet_chips, 0)

    live = jnp.concatenate(
        [(iota((1, CAP), 1) < counts_ref[0, 0, k]).astype(F32) for k in range(TILES)], axis=1
    )
    noise = flat(noise_ref[0, 0])
    start = live * flat(observed_ref[0, 0])
    weights_x = cubic_weights(flat(offsets_ref[0, 0, 0]))
    weights_y = cubic_weights(flat(offsets_ref[1, 0, 0]))
    weights_t = cubic_weights(flat(offsets_ref[2, 0, 0]))
    first_x = flat(cells_ref[0, 0, 0]) - XS * block_x
    first_y = flat(cells_ref[1, 0, 0]) - YS * block_y
    first_t = flat(cells_ref[2, 0, 0]) - 1
    rows_y = spread_rows(weights_y, first_y, iota((YS, SLOTS), 0) + 1)
    for x in range(7):
        row_x = spread_rows(weights_x, first_x, jnp.full((1, SLOTS), x, jnp.int32))
        plane[x * YS : (x + 1) * YS, :] = (row_x * rows_y).astype(BF16)
    edge_row = iota((YS, SLOTS), 0)
    edge_x = third(edge_row)
    edge_y = edge_row - 3 * edge_x
    edge_y = jnp.where(edge_y == 0, 0, YS + edge_y)
    plane[7 * YS :, :] = (
        spread_rows(weights_x, first_x, edge_x) * spread_rows(weights_y, first_y, edge_y)
    ).astype(BF16)
    rows_t = spread_rows(weights_t, first_t, iota((NT, SLOTS), 0)) * live
    time_rows[...] = rows_t
    high = rows_t.astype(BF16)
    low = (rows_t - high.astype(F32)).astype(BF16)
    kt = kt_ref[...]
    mixed_rows[...] = dot(kt, high) + dot(kt, low)

    edge_index = iota((NY, NY), 0)
    slot = edge_index & 63
    slot_x = third(slot)
    slot_y = slot - 3 * slot_x
    cell_y = (edge_index >> 6) * YS + jnp.where(slot_y == 0, -1, YS - 1 + slot_y)
    cell_y = jnp.where(slot < 21, cell_y, -1)
    select[...] = (cell_y == iota((NY, NY), 1)).astype(F32).astype(BF16)
    ky = ky_ref[...]
    mix_y[:NY, :] = ky
    mix_y[NY:, :] = dot(select[...], ky).astype(BF16)
    wide_row = iota((NY, NX), 0)
    wide_x = 2 * (wide_row & 3) + ((wide_row >> 2) & 1)
    cell_x = (wide_row >> 3) * XS - 1 + wide_x
    cell_x = jnp.where(wide_x < 7, cell_x, -1)
    widen = (cell_x == iota((NY, NX), 1)).astype(F32).astype(BF16)
    kx = kx_ref[...]
    mix_x[...] = dot_rows(dot(widen, kx).astype(BF16), widen).astype(BF16)

    def largest_sum(matrix):
        return jnp.max(
            jnp.sum(jnp.abs(matrix.astype(F32)), axis=0, keepdims=True), axis=1, keepdims=True
        )

    scale = 1.0 / (1.0 + largest_sum(kx) * largest_sum(ky) * largest_sum(kt))

    low_half = iota((32, 128), 1) < 64
    edge_lane = third(iota((8, NY), 1) & 63)

    pl.semaphore_wait(barrier, GROUP - 1 + CHIPS - 1)

    def wait_bytes(ref, count, semaphore):
        block = ref.at[pl.ds(0, count)]
        pltpu.make_async_copy(block, block, semaphore).wait()

    def apply_operator(turn_index, vector):
        weighted = (mixed_rows[...] * vector).astype(BF16)
        spread = dot_rows(weighted, plane[...])
        outgoing = jnp.concatenate(
            [
                spread[:, 128 * pair : 128 * (pair + 1)].reshape(GROUP, 8, 128)
                for pair in range(4)
            ],
            axis=1,
        ).astype(BF16)
        send_a[turn_index] = outgoing

        def start_a(step, carry):
            other = (member + step) % GROUP
            pltpu.make_async_remote_copy(
                src_ref=send_a.at[turn_index, other],
                dst_ref=recv_a.at[turn_index, member],
                send_sem=send_sem.at[turn_index, 0],
                recv_sem=recv_sem.at[turn_index, 0],
                device_id=group_device(other),
                device_id_type=MESH,
            ).start()
            return carry

        lax.fori_loop(1, GROUP, start_a, 0)
        recv_a[turn_index, member] = send_a[turn_index, member]
        wait_bytes(recv_a.at[turn_index], GROUP - 1, recv_sem.at[turn_index, 0])

        columns = []
        for pair in range(4):
            evens, odds = [], []
            for half in range(2):
                lower = recv_a[turn_index, 4 * pair + half].astype(F32)
                upper = recv_a[turn_index, 4 * pair + 2 + half].astype(F32)
                even = jnp.where(low_half, lower, pltpu.roll(upper, 64, 1))
                odd = jnp.where(low_half, pltpu.roll(lower, 64, 1), upper)
                evens.append(even)
                odds.append(odd)
            columns.append(jnp.concatenate([evens[0], odds[0], evens[1], odds[1]], axis=0))
        main = jnp.concatenate(columns, axis=1)
        zero = jnp.zeros((8, NY), F32)
        main_parts, edge_parts = [], []
        for half in range(2):
            edge = main[64 * half + 56 : 64 * half + 64, :]
            main_parts.append(main[64 * half : 64 * half + 56, :])
            main_parts.append(zero)
            for row in range(7):
                x = 2 * (row % 4) + row // 4
                edge_parts.append(jnp.where(edge_lane == x, edge, 0.0))
            edge_parts.append(zero)
        left = jnp.concatenate(
            [jnp.concatenate(main_parts, axis=0), jnp.concatenate(edge_parts, axis=0)], axis=1
        ).astype(BF16)
        mixed = dot(left, mix_y[...])

        for row in range(16):
            for quarter in range(4):
                turn[quarter, pl.ds(row, 8, stride=16), :] = mixed[
                    8 * row : 8 * row + 8, 128 * quarter : 128 * (quarter + 1)
                ]
        for quarter in range(4):
            send_b[turn_index, :, quarter] = turn[quarter].reshape(8, 16, 128).astype(BF16)

        def start_b(step, carry):
            other = (chip + step) % CHIPS
            pltpu.make_async_remote_copy(
                src_ref=send_b.at[turn_index, other // 4, other % 4],
                dst_ref=recv_b.at[turn_index, chip],
                send_sem=send_sem.at[turn_index, 1],
                recv_sem=recv_sem.at[turn_index, 1],
                device_id=chip_device(other),
                device_id_type=MESH,
            ).start()
            return carry

        lax.fori_loop(1, CHIPS, start_b, 0)
        recv_b[turn_index, chip] = send_b[turn_index, chip // 4, chip % 4]
        wait_bytes(recv_b.at[turn_index], CHIPS - 1, recv_sem.at[turn_index, 1])

        field = dot(mix_x[...], recv_b[turn_index].reshape(NY, 128))
        send_c[turn_index] = field.astype(BF16).reshape(CHIPS, 16, 128)

        def start_c(step, carry):
            other = (chip + step) % CHIPS
            pltpu.make_async_remote_copy(
                src_ref=send_c.at[turn_index, other],
                dst_ref=recv_c.at[turn_index, chip],
                send_sem=send_sem.at[turn_index, 2],
                recv_sem=recv_sem.at[turn_index, 2],
                device_id=chip_device(other),
                device_id_type=MESH,
            ).start()
            return carry

        lax.fori_loop(1, CHIPS, start_c, 0)
        recv_c[turn_index, chip] = send_c[turn_index, chip]
        wait_bytes(recv_c.at[turn_index], CHIPS - 1, recv_sem.at[turn_index, 2])

        for time in range(8):
            for quarter in range(4):
                turn[quarter, 16 * time : 16 * time + 16, :] = recv_c[
                    turn_index, 4 * time + quarter
                ].astype(F32)
        rows = [
            jnp.concatenate(
                [
                    turn[quarter, pl.ds(row, 8, stride=16), :]
                    for quarter in range(4)
                ],
                axis=1,
            )
            for row in range(16)
        ]
        edges = dot_rows(jnp.concatenate(rows, axis=0).astype(BF16), select[...])
        for half in range(2):
            edge = jnp.zeros((8, NY), F32)
            for row in range(7):
                x = 2 * (row % 4) + row // 4
                first = 64 * half + 8 * row
                edge = edge + jnp.where(edge_lane == x, edges[first : first + 8, :], 0.0)
            even = jnp.concatenate(rows[8 * half : 8 * half + 4], axis=0)
            odd = jnp.concatenate(rows[8 * half + 4 : 8 * half + 7] + [edge], axis=0)
            for pair in range(4):
                lanes = slice(128 * pair, 128 * (pair + 1))
                lower = jnp.where(low_half, even[:, lanes], pltpu.roll(odd[:, lanes], 64, 1))
                upper = jnp.where(low_half, pltpu.roll(even[:, lanes], 64, 1), odd[:, lanes])
                send_d[turn_index, 4 * pair + half] = lower.astype(BF16)
                send_d[turn_index, 4 * pair + 2 + half] = upper.astype(BF16)

        def start_d(step, carry):
            other = (member + step) % GROUP
            pltpu.make_async_remote_copy(
                src_ref=send_d.at[turn_index, other],
                dst_ref=recv_d.at[turn_index, member],
                send_sem=send_sem.at[turn_index, 3],
                recv_sem=recv_sem.at[turn_index, 3],
                device_id=group_device(other),
                device_id_type=MESH,
            ).start()
            return carry

        lax.fori_loop(1, GROUP, start_d, 0)
        recv_d[turn_index, member] = send_d[turn_index, member]
        wait_bytes(recv_d.at[turn_index], GROUP - 1, recv_sem.at[turn_index, 3])

        arrived = recv_d[turn_index].astype(F32)
        around = jnp.concatenate(
            [arrived[:, 8 * pair : 8 * pair + 8, :].reshape(NT, 128) for pair in range(4)], axis=1
        ).astype(BF16)
        picked = dot(around, plane[...])
        interpolated = jnp.sum(picked * time_rows[...], axis=0, keepdims=True)
        return scale * (interpolated + noise * vector)

    once = apply_operator(0, start)
    twice = apply_operator(1, once)

    products = jnp.concatenate(
        [
            start * start,
            start * once,
            once * once,
            start * twice,
            once * twice,
            jnp.zeros((3, SLOTS), F32),
        ],
        axis=0,
    )
    partial = products[:, :128]
    for part in range(1, 8):
        partial = partial + products[:, 128 * part : 128 * (part + 1)]
    sums[0] = partial
    sums_group[member] = partial

    def start_sum_group(step, carry):
        other = (member + step) % GROUP
        pltpu.make_async_remote_copy(
            src_ref=sums.at[0],
            dst_ref=sums_group.at[member],
            send_sem=sum_send_sem.at[0],
            recv_sem=sum_recv_sem.at[0],
            device_id=group_device(other),
            device_id_type=MESH,
        ).start()
        return carry

    lax.fori_loop(1, GROUP, start_sum_group, 0)
    wait_bytes(sums_group, GROUP - 1, sum_recv_sem.at[0])
    partial = jnp.sum(sums_group[...], axis=0)
    sums[1] = partial
    sums_chips[chip] = partial

    def start_sum_chips(step, carry):
        other = (chip + step) % CHIPS
        pltpu.make_async_remote_copy(
            src_ref=sums.at[1],
            dst_ref=sums_chips.at[chip],
            send_sem=sum_send_sem.at[1],
            recv_sem=sum_recv_sem.at[1],
            device_id=chip_device(other),
            device_id_type=MESH,
        ).start()
        return carry

    lax.fori_loop(1, CHIPS, start_sum_chips, 0)
    wait_bytes(sums_chips, CHIPS - 1, sum_recv_sem.at[1])
    totals = jnp.sum(jnp.sum(sums_chips[...], axis=0), axis=1, keepdims=True)
    rr, v0_v1, v1_v1, v0_v2, v1_v2 = [totals[k : k + 1, :] for k in range(5)]
    step_0 = rr / v0_v1
    ratio = step_0 * (v1_v1 / v0_v1)
    new = rr * (ratio - 1.0)
    direction = ratio * start - step_0 * once
    image = ratio * once - step_0 * twice
    curvature = ratio * ratio * v0_v1 - ratio * step_0 * (v1_v1 + v0_v2) + step_0 * step_0 * v1_v2
    step_1 = new / curvature
    solved = scale * (step_0 * start + step_1 * direction)
    rest = start - step_0 * once - step_1 * image
    for k in range(TILES):
        solution_ref[0, 0, k : k + 1, :] = solved[:, CAP * k : CAP * (k + 1)]
        residual_ref[0, 0, k : k + 1, :] = rest[:, CAP * k : CAP * (k + 1)]

    for turn_index in range(ITERS):
        wait_bytes(send_a.at[turn_index], GROUP - 1, send_sem.at[turn_index, 0])
        wait_bytes(recv_b.at[turn_index], CHIPS - 1, send_sem.at[turn_index, 1])
        wait_bytes(send_c.at[turn_index], CHIPS - 1, send_sem.at[turn_index, 2])
        wait_bytes(send_d.at[turn_index], GROUP - 1, send_sem.at[turn_index, 3])
    wait_bytes(sums_group, GROUP - 1, sum_send_sem.at[0])
    wait_bytes(sums_chips, CHIPS - 1, sum_send_sem.at[1])


def per_device(cells, offsets, counts, observed, noise, kernel_x, kernel_y, kernel_t):
    vmem = pl.BlockSpec(memory_space=pltpu.VMEM)
    group_block = (ITERS, GROUP, 32, 128)
    chip_block = (ITERS, CHIPS, 16, 128)
    return pl.pallas_call(
        kernel,
        out_shape=[jax.ShapeDtypeStruct(observed.shape, F32)] * 2,
        in_specs=[vmem, vmem, pl.BlockSpec(memory_space=pltpu.SMEM)] + [vmem] * 5,
        out_specs=[vmem, vmem],
        scratch_shapes=[
            pltpu.VMEM((NY, SLOTS), BF16),
            pltpu.VMEM((NT, SLOTS), F32),
            pltpu.VMEM((NT, SLOTS), F32),
            pltpu.VMEM((2 * NY, NY), BF16),
            pltpu.VMEM((NY, NY), BF16),
            pltpu.VMEM((NY, NY), BF16),
            pltpu.VMEM((4, NT, 128), F32),
            pltpu.VMEM(group_block, BF16),
            pltpu.VMEM(group_block, BF16),
            pltpu.VMEM((ITERS, 8, 4, 16, 128), BF16),
            pltpu.VMEM(chip_block, BF16),
            pltpu.VMEM(chip_block, BF16),
            pltpu.VMEM(chip_block, BF16),
            pltpu.VMEM(group_block, BF16),
            pltpu.VMEM(group_block, BF16),
            pltpu.VMEM((2, 8, 128), F32),
            pltpu.VMEM((GROUP, 8, 128), F32),
            pltpu.VMEM((CHIPS, 8, 128), F32),
            pltpu.SemaphoreType.DMA((ITERS, 4)),
            pltpu.SemaphoreType.DMA((ITERS, 4)),
            pltpu.SemaphoreType.DMA((2,)),
            pltpu.SemaphoreType.DMA((2,)),
        ],
        compiler_params=pltpu.CompilerParams(
            collective_id=0, has_side_effects=True, vmem_limit_bytes=48 * 1024 * 1024
        ),
    )(cells, offsets, counts, observed, noise, kernel_x, kernel_y, kernel_t)


def solution(mesh):
    placed = (
        P(None, "gx", "gy", None, None),
        P(None, "gx", "gy", None, None),
        P("gx", "gy", None),
        P("gx", "gy", None, None),
        P("gx", "gy", None, None),
        P(),
        P(),
        P(),
    )
    return jax.shard_map(
        per_device,
        mesh=mesh,
        in_specs=placed,
        out_specs=(P("gx", "gy", None, None), P("gx", "gy", None, None)),
        check_vma=False,
    )
```

```python
import jax
import jax.numpy as jnp
from jax import lax
from jax.experimental import pallas as pl
from jax.experimental.pallas import tpu as pltpu
from jax.sharding import PartitionSpec as P

XS = 4
YS = 64
ITERS = 2
TILES = 4
CAP = 256
SLOTS = TILES * CAP
CHIPS = 32
GROUP = 16
NX = 256
NY = 512
NT = 128
F32 = jnp.float32
BF16 = jnp.bfloat16
MESH = pl.DeviceIdType.MESH
ROW_ROW = (((1,), (1,)), ((), ()))
FAR_X = (2, 1, 3, 0)


def cubic_weights(fraction):
    square = fraction * fraction
    cubic_term = square * fraction
    return (
        (2.0 * square - cubic_term - fraction) * 0.5,
        (3.0 * cubic_term - 5.0 * square + 2.0) * 0.5,
        (4.0 * square - 3.0 * cubic_term + fraction) * 0.5,
        (cubic_term - square) * 0.5,
    )


def iota(shape, axis):
    return lax.broadcasted_iota(jnp.int32, shape, axis)


def flat(rows):
    return jnp.concatenate([rows[k : k + 1, :] for k in range(TILES)], axis=1)


def dot(left, right):
    return jnp.dot(left, right, preferred_element_type=F32)


def dot_rows(left, right):
    return lax.dot_general(left, right, ROW_ROW, preferred_element_type=F32)


def spread_rows(weights, first, rows):
    total = jnp.zeros(rows.shape, F32)
    for shift in range(4):
        total = total + jnp.where(first + shift == rows, weights[shift], 0.0)
    return total


def third(index):
    return (index * 43) >> 7


def lane_sum(row):
    total = row[:, :128]
    for part in range(1, SLOTS // 128):
        total = total + row[:, 128 * part : 128 * (part + 1)]
    return total


def sum_tile(*rows):
    return jnp.concatenate([*rows, jnp.zeros((8 - len(rows), 128), F32)], axis=0)


def totals_of(tile, count):
    totals = jnp.sum(tile, axis=1, keepdims=True)
    return [totals[k : k + 1, :] for k in range(count)]


def kernel(
    cells_hbm,
    offsets_hbm,
    counts_hbm,
    observed_hbm,
    noise_hbm,
    kx_hbm,
    ky_hbm,
    kt_hbm,
    solution_ref,
    residual_ref,
    cells_ref,
    offsets_ref,
    counts_ref,
    observed_ref,
    noise_ref,
    kx_ref,
    ky_ref,
    kt_ref,
    plane,
    time_rows,
    mixed_rows,
    mix_y,
    mix_x,
    select,
    turn,
    send_a,
    recv_a,
    send_b,
    recv_b,
    send_c,
    recv_c,
    send_d,
    recv_d,
    send_ga,
    recv_ga,
    send_gb,
    recv_gb,
    sum_first,
    sum_second,
    sum_group,
    sum_chips,
    load_sem,
    send_sem,
    recv_sem,
    sum_send_sem,
    sum_recv_sem,
):
    block_x = lax.axis_index("gx")
    block_y = lax.axis_index("gy")
    chip = block_x // 2
    core = block_x % 2
    chip_x = chip // 8
    chip_y = chip % 8
    member = block_y * 2 + core

    def far(step):
        return 4 + (step // 2) * (1 - step % 2) - ((step + 1) // 2) * (step % 2)

    def each_of_group(act):
        def one(step, carry):
            z = (block_y + far(step)) % 8
            for other_core in range(2):
                act(z * 2 + other_core, (chip * 2 + other_core, z))
            return carry

        lax.fori_loop(0, 7, one, 0)
        act(block_y * 2 + 1 - core, (chip * 2 + 1 - core, block_y))

    def each_of_chips(act):
        def one(step, carry):
            y = (chip_y + far(step)) % 8
            for shift in FAR_X:
                place = (chip_x + shift) % 4 * 8 + y
                act(place, (place * 2 + core, block_y))
            return carry

        lax.fori_loop(0, 7, one, 0)
        for shift in FAR_X[:3]:
            place = (chip_x + shift) % 4 * 8 + chip_y
            act(place, (place * 2 + core, block_y))

    barrier = pltpu.get_barrier_semaphore()

    def greet(place, device):
        pl.semaphore_signal(barrier, inc=1, device_id=device, device_id_type=MESH)

    loads = [
        pltpu.make_async_copy(source, target, load_sem.at[k])
        for k, (source, target) in enumerate(
            (
                (cells_hbm, cells_ref),
                (offsets_hbm, offsets_ref),
                (counts_hbm, counts_ref),
                (observed_hbm, observed_ref),
                (noise_hbm, noise_ref),
                (kt_hbm, kt_ref),
                (ky_hbm, ky_ref),
                (kx_hbm, kx_ref),
            )
        )
    ]
    for load in loads:
        load.start()
    each_of_chips(greet)
    each_of_group(greet)
    for load in loads[:6]:
        load.wait()

    live = jnp.concatenate(
        [
            (iota((1, CAP), 1) < counts_ref[0, :, k : k + 1]).astype(F32)
            for k in range(TILES)
        ],
        axis=1,
    )
    noise = flat(noise_ref[0, 0])
    start = live * flat(observed_ref[0, 0])
    weights_x = cubic_weights(flat(offsets_ref[0, 0, 0]))
    weights_y = cubic_weights(flat(offsets_ref[1, 0, 0]))
    weights_t = cubic_weights(flat(offsets_ref[2, 0, 0]))
    first_x = flat(cells_ref[0, 0, 0]) - XS * block_x
    first_y = flat(cells_ref[1, 0, 0]) - YS * block_y
    first_t = flat(cells_ref[2, 0, 0]) - 1
    rows_y = spread_rows(weights_y, first_y, iota((YS, SLOTS), 0) + 1)
    for x in range(7):
        row_x = spread_rows(weights_x, first_x, jnp.full((1, SLOTS), x, jnp.int32))
        plane[x * YS : (x + 1) * YS, :] = (row_x * rows_y).astype(BF16)
    edge_row = iota((YS, SLOTS), 0)
    edge_x = third(edge_row)
    edge_y = edge_row - 3 * edge_x
    edge_y = jnp.where(edge_y == 0, 0, YS + edge_y)
    plane[7 * YS :, :] = (
        spread_rows(weights_x, first_x, edge_x) * spread_rows(weights_y, first_y, edge_y)
    ).astype(BF16)
    rows_t = spread_rows(weights_t, first_t, iota((NT, SLOTS), 0)) * live
    time_rows[...] = rows_t
    high = rows_t.astype(BF16)
    low = (rows_t - high.astype(F32)).astype(BF16)
    kt = kt_ref[...]
    mixed_rows[...] = dot(kt, high) + dot(kt, low)

    low_half = iota((32, 128), 1) < 64
    edge_lane = third(iota((8, NY), 1) & 63)

    def wait_bytes(ref, count, semaphore):
        block = ref.at[pl.ds(0, count)]
        pltpu.make_async_copy(block, block, semaphore).wait()

    def copy_group(source, target, sent, received):
        def act(place, device):
            pltpu.make_async_remote_copy(
                src_ref=source(place),
                dst_ref=target.at[member],
                send_sem=sent,
                recv_sem=received,
                device_id=device,
                device_id_type=MESH,
            ).start()

        each_of_group(act)

    def copy_chips(source, target, sent, received):
        def act(place, device):
            pltpu.make_async_remote_copy(
                src_ref=source(place),
                dst_ref=target.at[chip],
                send_sem=sent,
                recv_sem=received,
                device_id=device,
                device_id_type=MESH,
            ).start()

        each_of_chips(act)

    def share_group(which, tile):
        source = sum_second if which != 1 else sum_first
        source[which] = tile
        sum_group[which, member] = tile
        copy_group(
            lambda place: source.at[which],
            sum_group.at[which],
            sum_send_sem.at[which, 0],
            sum_recv_sem.at[which, 0],
        )

    def share_chips(which, tile):
        source = sum_first if which != 1 else sum_second
        source[which] = tile
        sum_chips[which, chip] = tile
        copy_chips(
            lambda place: source.at[which],
            sum_chips.at[which],
            sum_send_sem.at[which, 1],
            sum_recv_sem.at[which, 1],
        )

    def shared_group(which):
        wait_bytes(sum_group.at[which], GROUP - 1, sum_recv_sem.at[which, 0])
        return jnp.sum(sum_group[which], axis=0)

    def shared_chips(which):
        wait_bytes(sum_chips.at[which], CHIPS - 1, sum_recv_sem.at[which, 1])
        return jnp.sum(sum_chips[which], axis=0)

    def time_blocks(spread):
        return jnp.concatenate(
            [
                spread[:, 128 * pair : 128 * (pair + 1)].reshape(GROUP, 8, 128)
                for pair in range(4)
            ],
            axis=1,
        ).astype(BF16)

    def whole_rows(received):
        columns = []
        for pair in range(4):
            parts = []
            for half in range(2):
                lower = received[4 * pair + half].astype(F32)
                upper = received[4 * pair + 2 + half].astype(F32)
                parts.append(jnp.where(low_half, lower, pltpu.roll(upper, 64, 1)))
                parts.append(jnp.where(low_half, pltpu.roll(lower, 64, 1), upper))
            columns.append(jnp.concatenate(parts, axis=0))
        main = jnp.concatenate(columns, axis=1)
        zero = jnp.zeros((8, NY), F32)
        main_parts, edge_parts = [], []
        for half in range(2):
            edge = main[64 * half + 56 : 64 * half + 64, :]
            main_parts.append(main[64 * half : 64 * half + 56, :])
            main_parts.append(zero)
            for row in range(7):
                x = 2 * (row % 4) + row // 4
                edge_parts.append(jnp.where(edge_lane == x, edge, 0.0))
            edge_parts.append(zero)
        return jnp.concatenate(main_parts, axis=0), jnp.concatenate(edge_parts, axis=0)

    def to_column_blocks(rows, target):
        for row in range(16):
            for quarter in range(4):
                turn[quarter, pl.ds(row, 8, stride=16), :] = rows[
                    8 * row : 8 * row + 8, 128 * quarter : 128 * (quarter + 1)
                ]
        for quarter in range(4):
            target[:, quarter] = turn[quarter].reshape(8, 16, 128).astype(BF16)

    def spread_out(turn_index, vector, tile):
        weighted = (mixed_rows[...] * vector).astype(BF16)
        send_a[turn_index] = time_blocks(dot_rows(weighted, plane[...]))
        if turn_index == 0:
            pl.semaphore_wait(barrier, GROUP - 1 + CHIPS - 1)
        copy_group(
            lambda place: send_a.at[turn_index, place],
            recv_a.at[turn_index],
            send_sem.at[turn_index, 0],
            recv_sem.at[turn_index, 0],
        )
        if tile is not None:
            share_group(1, tile)
        recv_a[turn_index, member] = send_a[turn_index, member]
        weighted = (time_rows[...] * vector).astype(BF16)
        send_ga[turn_index] = time_blocks(dot_rows(weighted, plane[...]))
        copy_group(
            lambda place: send_ga.at[turn_index, place],
            recv_ga.at[turn_index],
            send_sem.at[turn_index, 4],
            recv_sem.at[turn_index, 4],
        )
        recv_ga[turn_index, member] = send_ga[turn_index, member]

    def mix_along_y(turn_index):
        wait_bytes(recv_a.at[turn_index], GROUP - 1, recv_sem.at[turn_index, 0])
        main, edge = whole_rows(recv_a[turn_index])
        left = jnp.concatenate([main, edge], axis=1).astype(BF16)
        to_column_blocks(dot(left, mix_y[...]), send_b.at[turn_index])
        copy_chips(
            lambda place: send_b.at[turn_index, place // 4, place % 4],
            recv_b.at[turn_index],
            send_sem.at[turn_index, 1],
            recv_sem.at[turn_index, 1],
        )
        recv_b[turn_index, chip] = send_b[turn_index, chip // 4, chip % 4]
        if turn_index == 1:
            share_chips(1, shared_group(1))
        wait_bytes(recv_ga.at[turn_index], GROUP - 1, recv_sem.at[turn_index, 4])
        main, edge = whole_rows(recv_ga[turn_index])
        to_column_blocks(main + dot(edge.astype(BF16), select[...]), send_gb.at[turn_index])
        copy_chips(
            lambda place: send_gb.at[turn_index, place // 4, place % 4],
            recv_gb.at[turn_index],
            send_sem.at[turn_index, 5],
            recv_sem.at[turn_index, 5],
        )
        recv_gb[turn_index, chip] = send_gb[turn_index, chip // 4, chip % 4]

    def grid_columns(turn_index):
        wait_bytes(recv_b.at[turn_index], CHIPS - 1, recv_sem.at[turn_index, 1])
        return recv_b[turn_index].reshape(NY, 128)

    def spread_columns(turn_index):
        wait_bytes(recv_gb.at[turn_index], CHIPS - 1, recv_sem.at[turn_index, 5])
        return recv_gb[turn_index].reshape(NY, 128).astype(F32)

    def send_field(turn_index, field):
        send_c[turn_index] = field.astype(BF16).reshape(CHIPS, 16, 128)
        copy_chips(
            lambda place: send_c.at[turn_index, place],
            recv_c.at[turn_index],
            send_sem.at[turn_index, 2],
            recv_sem.at[turn_index, 2],
        )
        recv_c[turn_index, chip] = send_c[turn_index, chip]

    def field_back(turn_index, which):
        wait_bytes(recv_c.at[turn_index], CHIPS - 1, recv_sem.at[turn_index, 2])
        for time in range(8):
            for quarter in range(4):
                turn[quarter, 16 * time : 16 * time + 16, :] = recv_c[
                    turn_index, 4 * time + quarter
                ].astype(F32)
        rows = [
            jnp.concatenate(
                [turn[quarter, pl.ds(row, 8, stride=16), :] for quarter in range(4)], axis=1
            )
            for row in range(16)
        ]
        edges = dot_rows(jnp.concatenate(rows, axis=0).astype(BF16), select[...])
        for half in range(2):
            edge = jnp.zeros((8, NY), F32)
            for row in range(7):
                x = 2 * (row % 4) + row // 4
                first = 64 * half + 8 * row
                edge = edge + jnp.where(edge_lane == x, edges[first : first + 8, :], 0.0)
            even = jnp.concatenate(rows[8 * half : 8 * half + 4], axis=0)
            odd = jnp.concatenate(rows[8 * half + 4 : 8 * half + 7] + [edge], axis=0)
            for pair in range(4):
                lanes = slice(128 * pair, 128 * (pair + 1))
                lower = jnp.where(low_half, even[:, lanes], pltpu.roll(odd[:, lanes], 64, 1))
                upper = jnp.where(low_half, pltpu.roll(even[:, lanes], 64, 1), odd[:, lanes])
                send_d[turn_index, 4 * pair + half] = lower.astype(BF16)
                send_d[turn_index, 4 * pair + 2 + half] = upper.astype(BF16)
        copy_group(
            lambda place: send_d.at[turn_index, place],
            recv_d.at[turn_index],
            send_sem.at[turn_index, 3],
            recv_sem.at[turn_index, 3],
        )
        recv_d[turn_index, member] = send_d[turn_index, member]
        share_group(which, shared_chips(which))
        wait_bytes(recv_d.at[turn_index], GROUP - 1, recv_sem.at[turn_index, 3])
        arrived = recv_d[turn_index].astype(F32)
        around = jnp.concatenate(
            [arrived[:, 8 * pair : 8 * pair + 8, :].reshape(NT, 128) for pair in range(4)], axis=1
        ).astype(BF16)
        picked = dot(around, plane[...])
        return jnp.sum(picked * time_rows[...], axis=0, keepdims=True)

    spread_out(0, start, None)

    for load in loads[6:]:
        load.wait()
    edge_index = iota((NY, NY), 0)
    slot = edge_index & 63
    slot_x = third(slot)
    slot_y = slot - 3 * slot_x
    cell_y = (edge_index >> 6) * YS + jnp.where(slot_y == 0, -1, YS - 1 + slot_y)
    cell_y = jnp.where(slot < 21, cell_y, -1)
    select[...] = (cell_y == iota((NY, NY), 1)).astype(F32).astype(BF16)
    ky = ky_ref[...]
    mix_y[:NY, :] = ky
    mix_y[NY:, :] = dot(select[...], ky).astype(BF16)
    wide_row = iota((NY, NX), 0)
    wide_x = 2 * (wide_row & 3) + ((wide_row >> 2) & 1)
    cell_x = (wide_row >> 3) * XS - 1 + wide_x
    cell_x = jnp.where(wide_x < 7, cell_x, -1)
    widen = (cell_x == iota((NY, NX), 1)).astype(F32).astype(BF16)
    mix_x[...] = dot_rows(dot(widen, kx_ref[...]).astype(BF16), widen).astype(BF16)

    mix_along_y(0)
    field = dot(mix_x[...], grid_columns(0))
    send_field(0, field)
    inner = jnp.sum(field * spread_columns(0), axis=0, keepdims=True)
    share_chips(0, sum_tile(lane_sum(start * start), lane_sum(noise * start * start), inner))
    interpolated = field_back(0, 0)
    rr, noise_00, inner = totals_of(shared_group(0), 3)
    step_0 = rr / (inner + noise_00)
    rest = start - step_0 * (interpolated + noise * start)

    spread_out(
        1,
        rest,
        sum_tile(
            lane_sum(rest * rest), lane_sum(noise * rest * rest), lane_sum(noise * rest * start)
        ),
    )
    mix_along_y(1)
    columns = grid_columns(1).astype(F32)
    new, noise_11, noise_01 = totals_of(shared_chips(1), 3)
    ratio = new / rr
    columns = columns + ratio * recv_b[0].reshape(NY, 128).astype(F32)
    field = dot(mix_x[...], columns.astype(BF16))
    send_field(1, field)
    both = spread_columns(1) + ratio * recv_gb[0].reshape(NY, 128).astype(F32)
    share_chips(2, sum_tile(jnp.sum(field * both, axis=0, keepdims=True)))
    interpolated = field_back(1, 2)
    (inner,) = totals_of(shared_group(2), 1)
    curvature = inner + noise_11 + ratio * (2.0 * noise_01 + ratio * noise_00)
    step_1 = new / curvature
    direction = rest + ratio * start
    solved = step_0 * start + step_1 * direction
    rest = rest - step_1 * (interpolated + noise * direction)
    for k in range(TILES):
        solution_ref[0, 0, k : k + 1, :] = solved[:, CAP * k : CAP * (k + 1)]
        residual_ref[0, 0, k : k + 1, :] = rest[:, CAP * k : CAP * (k + 1)]

    for turn_index in range(ITERS):
        wait_bytes(recv_a.at[turn_index], GROUP - 1, send_sem.at[turn_index, 0])
        wait_bytes(recv_b.at[turn_index], CHIPS - 1, send_sem.at[turn_index, 1])
        wait_bytes(recv_c.at[turn_index], CHIPS - 1, send_sem.at[turn_index, 2])
        wait_bytes(recv_d.at[turn_index], GROUP - 1, send_sem.at[turn_index, 3])
        wait_bytes(recv_ga.at[turn_index], GROUP - 1, send_sem.at[turn_index, 4])
        wait_bytes(recv_gb.at[turn_index], CHIPS - 1, send_sem.at[turn_index, 5])
    for which in range(3):
        wait_bytes(sum_group.at[which], GROUP - 1, sum_send_sem.at[which, 0])
        wait_bytes(sum_chips.at[which], CHIPS - 1, sum_send_sem.at[which, 1])


def per_device(cells, offsets, counts, observed, noise, kernel_x, kernel_y, kernel_t):
    vmem = pl.BlockSpec(memory_space=pltpu.VMEM)
    whole = pl.BlockSpec(memory_space=pltpu.HBM)
    group_block = pltpu.VMEM((ITERS, GROUP, 32, 128), BF16)
    chip_block = pltpu.VMEM((ITERS, CHIPS, 16, 128), BF16)
    time_block = pltpu.VMEM((ITERS, 8, 4, 16, 128), BF16)
    operands = (cells, offsets, counts, observed, noise, kernel_x, kernel_y, kernel_t)
    return pl.pallas_call(
        kernel,
        out_shape=[jax.ShapeDtypeStruct(observed.shape, F32)] * 2,
        in_specs=[whole] * 8,
        out_specs=[vmem, vmem],
        scratch_shapes=[pltpu.VMEM(operand.shape, operand.dtype) for operand in operands]
        + [
            pltpu.VMEM((NY, SLOTS), BF16),
            pltpu.VMEM((NT, SLOTS), F32),
            pltpu.VMEM((NT, SLOTS), F32),
            pltpu.VMEM((2 * NY, NY), BF16),
            pltpu.VMEM((NY, NY), BF16),
            pltpu.VMEM((NY, NY), BF16),
            pltpu.VMEM((4, NT, 128), F32),
            group_block,
            group_block,
            time_block,
            chip_block,
            chip_block,
            chip_block,
            group_block,
            group_block,
            group_block,
            group_block,
            time_block,
            chip_block,
            pltpu.VMEM((3, 8, 128), F32),
            pltpu.VMEM((3, 8, 128), F32),
            pltpu.VMEM((3, GROUP, 8, 128), F32),
            pltpu.VMEM((3, CHIPS, 8, 128), F32),
            pltpu.SemaphoreType.DMA((8,)),
            pltpu.SemaphoreType.DMA((ITERS, 6)),
            pltpu.SemaphoreType.DMA((ITERS, 6)),
            pltpu.SemaphoreType.DMA((3, 2)),
            pltpu.SemaphoreType.DMA((3, 2)),
        ],
        compiler_params=pltpu.CompilerParams(
            collective_id=0, has_side_effects=True, vmem_limit_bytes=63 * 1024 * 1024
        ),
    )(*operands)


def solution(mesh):
    placed = (
        P(None, "gx", "gy", None, None),
        P(None, "gx", "gy", None, None),
        P("gx", "gy", None),
        P("gx", "gy", None, None),
        P("gx", "gy", None, None),
        P(),
        P(),
        P(),
    )
    return jax.shard_map(
        per_device,
        mesh=mesh,
        in_specs=placed,
        out_specs=(P("gx", "gy", None, None), P("gx", "gy", None, None)),
        check_vma=False,
    )
```

```python
import jax
import jax.numpy as jnp
from jax import lax
from jax.experimental import pallas as pl
from jax.experimental.pallas import tpu as pltpu
from jax.sharding import PartitionSpec as P

XS = 4
YS = 64
ITERS = 2
TILES = 4
CAP = 256
SLOTS = TILES * CAP
CHIPS = 32
GROUP = 16
NX = 256
NY = 512
NT = 128
F32 = jnp.float32
BF16 = jnp.bfloat16
MESH = pl.DeviceIdType.MESH
ROW_ROW = (((1,), (1,)), ((), ()))
FAR_X = (2, 1, 3, 0)
FREE = 88


def cubic_weights(fraction):
    square = fraction * fraction
    cubic_term = square * fraction
    return (
        (2.0 * square - cubic_term - fraction) * 0.5,
        (3.0 * cubic_term - 5.0 * square + 2.0) * 0.5,
        (4.0 * square - 3.0 * cubic_term + fraction) * 0.5,
        (cubic_term - square) * 0.5,
    )


def iota(shape, axis):
    return lax.broadcasted_iota(jnp.int32, shape, axis)


def flat(rows):
    return jnp.concatenate([rows[k : k + 1, :] for k in range(TILES)], axis=1)


def dot(left, right):
    return jnp.dot(left, right, preferred_element_type=F32)


def dot_rows(left, right):
    return lax.dot_general(left, right, ROW_ROW, preferred_element_type=F32)


def spread_rows(weights, first, rows):
    total = jnp.zeros(rows.shape, F32)
    for shift in range(4):
        total = total + jnp.where(first + shift == rows, weights[shift], 0.0)
    return total


def third(index):
    return (index * 43) >> 7


def lane_sum(row):
    total = row[:, :128]
    for part in range(1, SLOTS // 128):
        total = total + row[:, 128 * part : 128 * (part + 1)]
    return total


def sum_row(*rows):
    lanes = iota((1, 128), 1)
    total = jnp.zeros((1, 128), F32)
    for k, row in enumerate(rows):
        total = jnp.where(lanes == FREE + k, jnp.sum(row, axis=1, keepdims=True), total)
    return total


def totals_of(row, count):
    return [
        jnp.sum(jnp.where(iota(row.shape, 1) == FREE + k, row, 0.0), axis=1, keepdims=True)
        for k in range(count)
    ]


def pieces(row):
    high = row.astype(BF16).astype(F32)
    middle = (row - high).astype(BF16).astype(F32)
    return high, middle, (row - high - middle).astype(BF16).astype(F32)


def group_tile(row):
    rows = iota((8, 128), 0)
    tile = jnp.zeros((8, 128), F32)
    for k, piece in enumerate(pieces(row)):
        tile = jnp.where(rows == k, piece, tile)
    return tile


def chip_tile(row):
    high, middle, low = pieces(row)
    rows = iota((16, 128), 0)
    tile = jnp.where(rows == 7, high + pltpu.roll(low, 8, 1), 0.0)
    return jnp.where(rows == 15, middle, tile)


def group_rows(received):
    rows = []
    for member in range(GROUP):
        tile = received[member, 16:, :].astype(F32)
        rows.append(tile[8:9, :] + tile[9:10, :] + tile[10:11, :])
    return jnp.concatenate(rows, axis=0)


def chip_rows(received):
    rows = []
    for chip in range(CHIPS):
        tile = received[chip].astype(F32)
        rows.append(tile[7:8, :] + tile[15:16, :] + pltpu.roll(tile[7:8, :], 120, 1))
    return jnp.concatenate(rows, axis=0)


def quotient(above, below):
    return jnp.where(below > 0.0, above / jnp.where(below > 0.0, below, 1.0), 0.0)


def kernel(
    cells_hbm,
    offsets_hbm,
    counts_hbm,
    observed_hbm,
    noise_hbm,
    kx_hbm,
    ky_hbm,
    kt_hbm,
    solution_ref,
    residual_ref,
    cells_ref,
    offsets_ref,
    counts_ref,
    observed_ref,
    noise_ref,
    kx_ref,
    ky_ref,
    kt_ref,
    plane,
    time_rows,
    mixed_rows,
    mix_y,
    mix_x,
    select,
    turn,
    send_a,
    recv_a,
    send_b,
    recv_b,
    send_c,
    recv_c,
    send_d,
    recv_d,
    send_ga,
    recv_ga,
    send_gb,
    recv_gb,
    sums_sent,
    sums_chips,
    sums_group,
    load_sem,
    send_sem,
    recv_sem,
    plain_sem,
    sum_sem,
):
    block_x = lax.axis_index("gx")
    block_y = lax.axis_index("gy")
    chip = block_x // 2
    core = block_x % 2
    chip_x = chip // 8
    chip_y = chip % 8
    member = block_y * 2 + core

    def far(step):
        return 4 + (step // 2) * (1 - step % 2) - ((step + 1) // 2) * (step % 2)

    def each_of_group(act):
        def one(step, carry):
            z = (block_y + far(step)) % 8
            for other_core in range(2):
                act(z * 2 + other_core, (chip * 2 + other_core, z))
            return carry

        lax.fori_loop(0, 7, one, 0)
        act(block_y * 2 + 1 - core, (chip * 2 + 1 - core, block_y))

    def each_of_chips(act):
        def one(step, carry):
            y = (chip_y + far(step)) % 8
            for shift in FAR_X:
                place = (chip_x + shift) % 4 * 8 + y
                act(place, (place * 2 + core, block_y))
            return carry

        lax.fori_loop(0, 7, one, 0)
        for shift in FAR_X[:3]:
            place = (chip_x + shift) % 4 * 8 + chip_y
            act(place, (place * 2 + core, block_y))

    barrier = pltpu.get_barrier_semaphore()

    def greet(place, device):
        pl.semaphore_signal(barrier, inc=1, device_id=device, device_id_type=MESH)

    loads = [
        pltpu.make_async_copy(source, target, load_sem.at[k])
        for k, (source, target) in enumerate(
            (
                (cells_hbm, cells_ref),
                (offsets_hbm, offsets_ref),
                (counts_hbm, counts_ref),
                (observed_hbm, observed_ref),
                (noise_hbm, noise_ref),
                (kt_hbm, kt_ref),
                (ky_hbm, ky_ref),
                (kx_hbm, kx_ref),
            )
        )
    ]
    for load in loads:
        load.start()
    each_of_chips(greet)
    each_of_group(greet)
    for load in loads[:6]:
        load.wait()

    live = jnp.concatenate(
        [
            (iota((1, CAP), 1) < counts_ref[0, :, k : k + 1]).astype(F32)
            for k in range(TILES)
        ],
        axis=1,
    )
    noise = flat(noise_ref[0, 0])
    start = live * flat(observed_ref[0, 0])
    weights_x = cubic_weights(flat(offsets_ref[0, 0, 0]))
    weights_y = cubic_weights(flat(offsets_ref[1, 0, 0]))
    weights_t = cubic_weights(flat(offsets_ref[2, 0, 0]))
    first_x = flat(cells_ref[0, 0, 0]) - XS * block_x
    first_y = flat(cells_ref[1, 0, 0]) - YS * block_y
    first_t = flat(cells_ref[2, 0, 0]) - 1
    rows_y = spread_rows(weights_y, first_y, iota((YS, SLOTS), 0) + 1)
    for x in range(7):
        row_x = spread_rows(weights_x, first_x, jnp.full((1, SLOTS), x, jnp.int32))
        plane[x * YS : (x + 1) * YS, :] = (row_x * rows_y).astype(BF16)
    edge_row = iota((YS, SLOTS), 0)
    edge_x = third(edge_row)
    edge_y = edge_row - 3 * edge_x
    edge_y = jnp.where(edge_y == 0, 0, YS + edge_y)
    plane[7 * YS :, :] = (
        spread_rows(weights_x, first_x, edge_x) * spread_rows(weights_y, first_y, edge_y)
    ).astype(BF16)
    rows_t = spread_rows(weights_t, first_t, iota((NT, SLOTS), 0)) * live
    time_rows[...] = rows_t
    high = rows_t.astype(BF16)
    low = (rows_t - high.astype(F32)).astype(BF16)
    kt = kt_ref[...]
    mixed_rows[...] = dot(kt, high) + dot(kt, low)

    low_half = iota((32, 128), 1) < 64
    edge_lane = third(iota((8, NY), 1) & 63)

    def wait_bytes(ref, count, semaphore):
        block = ref.at[pl.ds(0, count)]
        pltpu.make_async_copy(block, block, semaphore).wait()

    def copy_group(source, target, sent, received):
        def act(place, device):
            pltpu.make_async_remote_copy(
                src_ref=source(place),
                dst_ref=target.at[member],
                send_sem=sent,
                recv_sem=received,
                device_id=device,
                device_id_type=MESH,
            ).start()

        each_of_group(act)

    def copy_chips(source, target, sent, received):
        def act(place, device):
            pltpu.make_async_remote_copy(
                src_ref=source(place),
                dst_ref=target.at[chip],
                send_sem=sent,
                recv_sem=received,
                device_id=device,
                device_id_type=MESH,
            ).start()

        each_of_chips(act)

    def time_blocks(spread, tile):
        blocks = [
            spread[:, 128 * pair : 128 * (pair + 1)].reshape(GROUP, 8, 128) for pair in range(4)
        ]
        if tile is not None:
            blocks[3] = blocks[3] + tile[None]
        return jnp.concatenate(blocks, axis=1).astype(BF16)

    def whole_rows(received):
        columns = []
        for pair in range(4):
            parts = []
            for half in range(2):
                lower = received[4 * pair + half]
                upper = received[4 * pair + 2 + half]
                parts.append(jnp.where(low_half, lower, pltpu.roll(upper, 64, 1)))
                parts.append(jnp.where(low_half, pltpu.roll(lower, 64, 1), upper))
            columns.append(jnp.concatenate(parts, axis=0))
        main = jnp.concatenate(columns, axis=1)
        zero = jnp.zeros((8, NY), F32)
        main_parts, edge_parts = [], []
        for half in range(2):
            edge = main[64 * half + 56 : 64 * half + 64, :]
            main_parts.append(main[64 * half : 64 * half + 56, :])
            main_parts.append(zero)
            for row in range(7):
                x = 2 * (row % 4) + row // 4
                edge_parts.append(jnp.where(edge_lane == x, edge, 0.0))
            edge_parts.append(zero)
        return jnp.concatenate(main_parts, axis=0), jnp.concatenate(edge_parts, axis=0)

    def to_column_blocks(rows, target, tile):
        for row in range(16):
            for quarter in range(4):
                turn[quarter, pl.ds(row, 8, stride=16), :] = rows[
                    8 * row : 8 * row + 8, 128 * quarter : 128 * (quarter + 1)
                ]
        for quarter in range(4):
            blocks = turn[quarter].reshape(8, 16, 128)
            if tile is not None:
                blocks = blocks + tile[None]
            target[:, quarter] = blocks.astype(BF16)

    def spread_out(turn_index, vector, tile):
        weighted = (mixed_rows[...] * vector).astype(BF16)
        send_a[turn_index] = time_blocks(dot_rows(weighted, plane[...]), tile)
        if turn_index == 0:
            pl.semaphore_wait(barrier, GROUP - 1 + CHIPS - 1)
        copy_group(
            lambda place: send_a.at[turn_index, place],
            recv_a.at[turn_index],
            send_sem.at[turn_index, 0],
            recv_sem.at[turn_index, 0],
        )
        recv_a[turn_index, member] = send_a[turn_index, member]

    def spread_plain(vector):
        weighted = (time_rows[...] * vector).astype(BF16)
        send_ga[...] = time_blocks(dot_rows(weighted, plane[...]), None)
        copy_group(lambda place: send_ga.at[place], recv_ga, plain_sem.at[0], plain_sem.at[1])
        recv_ga[member] = send_ga[member]

    def arrived_blocks(turn_index):
        wait_bytes(recv_a.at[turn_index], GROUP - 1, recv_sem.at[turn_index, 0])
        return [recv_a[turn_index, place].astype(F32) for place in range(GROUP)]

    def mix_along_y(turn_index, blocks, tile):
        main, edge = whole_rows(blocks)
        left = jnp.concatenate([main, edge], axis=1).astype(BF16)
        to_column_blocks(dot(left, mix_y[...]), send_b.at[turn_index], tile)
        copy_chips(
            lambda place: send_b.at[turn_index, place // 4, place % 4],
            recv_b.at[turn_index],
            send_sem.at[turn_index, 1],
            recv_sem.at[turn_index, 1],
        )
        recv_b[turn_index, chip] = send_b[turn_index, chip // 4, chip % 4]

    def fold_plain():
        wait_bytes(recv_ga, GROUP - 1, plain_sem.at[1])
        main, edge = whole_rows([recv_ga[place].astype(F32) for place in range(GROUP)])
        to_column_blocks(main + dot(edge.astype(BF16), select[...]), send_gb, None)
        copy_chips(
            lambda place: send_gb.at[place // 4, place % 4],
            recv_gb,
            plain_sem.at[2],
            plain_sem.at[3],
        )
        recv_gb[chip] = send_gb[chip // 4, chip % 4]

    def grid_columns(turn_index):
        wait_bytes(recv_b.at[turn_index], CHIPS - 1, recv_sem.at[turn_index, 1])
        return recv_b[turn_index].reshape(NY, 128)

    def spread_columns():
        wait_bytes(recv_gb, CHIPS - 1, plain_sem.at[3])
        return recv_gb[...].reshape(NY, 128).astype(F32)

    def send_field(turn_index, field):
        send_c[turn_index] = field.astype(BF16).reshape(CHIPS, 16, 128)
        copy_chips(
            lambda place: send_c.at[turn_index, place],
            recv_c.at[turn_index],
            send_sem.at[turn_index, 2],
            recv_sem.at[turn_index, 2],
        )
        recv_c[turn_index, chip] = send_c[turn_index, chip]

    def field_back(turn_index):
        wait_bytes(recv_c.at[turn_index], CHIPS - 1, recv_sem.at[turn_index, 2])
        for time in range(8):
            for quarter in range(4):
                turn[quarter, 16 * time : 16 * time + 16, :] = recv_c[
                    turn_index, 4 * time + quarter
                ].astype(F32)
        rows = [
            jnp.concatenate(
                [turn[quarter, pl.ds(row, 8, stride=16), :] for quarter in range(4)], axis=1
            )
            for row in range(16)
        ]
        edges = dot_rows(jnp.concatenate(rows, axis=0).astype(BF16), select[...])
        for half in range(2):
            edge = jnp.zeros((8, NY), F32)
            for row in range(7):
                x = 2 * (row % 4) + row // 4
                first = 64 * half + 8 * row
                edge = edge + jnp.where(edge_lane == x, edges[first : first + 8, :], 0.0)
            even = jnp.concatenate(rows[8 * half : 8 * half + 4], axis=0)
            odd = jnp.concatenate(rows[8 * half + 4 : 8 * half + 7] + [edge], axis=0)
            for pair in range(4):
                lanes = slice(128 * pair, 128 * (pair + 1))
                lower = jnp.where(low_half, even[:, lanes], pltpu.roll(odd[:, lanes], 64, 1))
                upper = jnp.where(low_half, pltpu.roll(even[:, lanes], 64, 1), odd[:, lanes])
                send_d[turn_index, 4 * pair + half] = lower.astype(BF16)
                send_d[turn_index, 4 * pair + 2 + half] = upper.astype(BF16)
        copy_group(
            lambda place: send_d.at[turn_index, place],
            recv_d.at[turn_index],
            send_sem.at[turn_index, 3],
            recv_sem.at[turn_index, 3],
        )
        recv_d[turn_index, member] = send_d[turn_index, member]

    def at_slots(turn_index):
        wait_bytes(recv_d.at[turn_index], GROUP - 1, recv_sem.at[turn_index, 3])
        arrived = recv_d[turn_index].astype(F32)
        around = jnp.concatenate(
            [arrived[:, 8 * pair : 8 * pair + 8, :].reshape(NT, 128) for pair in range(4)], axis=1
        ).astype(BF16)
        picked = dot(around, plane[...])
        return jnp.sum(picked * time_rows[...], axis=0, keepdims=True)

    spread_out(0, start, None)

    for load in loads[6:]:
        load.wait()
    edge_index = iota((NY, NY), 0)
    slot = edge_index & 63
    slot_x = third(slot)
    slot_y = slot - 3 * slot_x
    cell_y = (edge_index >> 6) * YS + jnp.where(slot_y == 0, -1, YS - 1 + slot_y)
    cell_y = jnp.where(slot < 21, cell_y, -1)
    select[...] = (cell_y == iota((NY, NY), 1)).astype(F32).astype(BF16)
    ky = ky_ref[...]
    mix_y[:NY, :] = ky
    mix_y[NY:, :] = dot(select[...], ky).astype(BF16)
    wide_row = iota((NY, NX), 0)
    wide_x = 2 * (wide_row & 3) + ((wide_row >> 2) & 1)
    cell_x = (wide_row >> 3) * XS - 1 + wide_x
    cell_x = jnp.where(wide_x < 7, cell_x, -1)
    widen = (cell_x == iota((NY, NX), 1)).astype(F32).astype(BF16)
    mix_x[...] = dot_rows(dot(widen, kx_ref[...]).astype(BF16), widen).astype(BF16)

    mix_along_y(0, arrived_blocks(0), None)
    send_field(0, dot(mix_x[...], grid_columns(0)))
    field_back(0)
    image_0 = at_slots(0) + noise * start

    sums = sum_row(
        lane_sum(start * start),
        lane_sum(start * image_0),
        lane_sum(image_0 * image_0),
        lane_sum(noise * start * image_0),
        lane_sum(noise * image_0 * image_0),
    )
    own = totals_of(sums, 2)
    spread_out(1, image_0 - quotient(own[1], own[0]) * start, group_tile(sums))
    spread_plain(image_0)
    blocks = arrived_blocks(1)
    member_sums = group_rows(recv_a[1])
    group_sums = jnp.sum(member_sums, axis=0, keepdims=True)
    members = totals_of(member_sums, 2)
    group = totals_of(group_sums, 2)
    part = quotient(members[1], members[0]) - quotient(group[1], group[0])
    blocks = [
        blocks[place] + part[place : place + 1, :] * recv_a[0, place].astype(F32)
        for place in range(GROUP)
    ]
    mix_along_y(1, blocks, chip_tile(group_sums))
    fold_plain()
    grid_columns(1)
    chip_sums = chip_rows(recv_b[1])
    chips = totals_of(chip_sums, 2)
    rr, along, square, noise_01, noise_11 = totals_of(
        jnp.sum(chip_sums, axis=0, keepdims=True), 5
    )
    step_0 = rr / along
    grow = step_0 * (square / along)
    ratio = jnp.maximum(grow - 1.0, 0.0)
    new = rr * ratio
    part = grow - step_0 * quotient(chips[1], chips[0])
    columns = jnp.concatenate(
        [
            part[place : place + 1, :] * recv_b[0, place].astype(F32)
            - step_0 * recv_b[1, place].astype(F32)
            for place in range(CHIPS)
        ],
        axis=0,
    )
    field = dot(mix_x[...], columns.astype(BF16))
    send_field(1, field)
    inner = jnp.sum(jnp.sum(field * spread_columns(), axis=0, keepdims=True), axis=1, keepdims=True)
    inner = jnp.broadcast_to(inner, (8, 128))
    sums_sent[0] = inner
    sums_chips[chip] = inner
    copy_chips(lambda place: sums_sent.at[0], sums_chips, sum_sem.at[0], sum_sem.at[1])
    field_back(1)
    wait_bytes(sums_chips, CHIPS - 1, sum_sem.at[1])
    inner = jnp.sum(sums_chips[...], axis=0)
    sums_sent[1] = inner
    sums_group[member] = inner
    copy_group(lambda place: sums_sent.at[1], sums_group, sum_sem.at[2], sum_sem.at[3])
    direction = grow * start - step_0 * image_0
    image_1 = at_slots(1) + noise * direction
    wait_bytes(sums_group, GROUP - 1, sum_sem.at[3])
    inner = jnp.sum(sums_group[...], axis=0)[:1, :1]
    curvature = -step_0 * (inner + grow * noise_01 - step_0 * noise_11)
    step_1 = new / curvature
    solved = step_0 * start + step_1 * direction
    rest = start - step_0 * image_0 - step_1 * image_1
    for k in range(TILES):
        solution_ref[0, 0, k : k + 1, :] = solved[:, CAP * k : CAP * (k + 1)]
        residual_ref[0, 0, k : k + 1, :] = rest[:, CAP * k : CAP * (k + 1)]

    for turn_index in range(ITERS):
        wait_bytes(recv_a.at[turn_index], GROUP - 1, send_sem.at[turn_index, 0])
        wait_bytes(recv_b.at[turn_index], CHIPS - 1, send_sem.at[turn_index, 1])
        wait_bytes(recv_c.at[turn_index], CHIPS - 1, send_sem.at[turn_index, 2])
        wait_bytes(recv_d.at[turn_index], GROUP - 1, send_sem.at[turn_index, 3])
    wait_bytes(recv_ga, GROUP - 1, plain_sem.at[0])
    wait_bytes(recv_gb, CHIPS - 1, plain_sem.at[2])
    wait_bytes(sums_chips, CHIPS - 1, sum_sem.at[0])
    wait_bytes(sums_group, GROUP - 1, sum_sem.at[2])


def per_device(cells, offsets, counts, observed, noise, kernel_x, kernel_y, kernel_t):
    vmem = pl.BlockSpec(memory_space=pltpu.VMEM)
    whole = pl.BlockSpec(memory_space=pltpu.HBM)
    group_block = pltpu.VMEM((ITERS, GROUP, 32, 128), BF16)
    chip_block = pltpu.VMEM((ITERS, CHIPS, 16, 128), BF16)
    time_block = pltpu.VMEM((ITERS, 8, 4, 16, 128), BF16)
    operands = (cells, offsets, counts, observed, noise, kernel_x, kernel_y, kernel_t)
    return pl.pallas_call(
        kernel,
        out_shape=[jax.ShapeDtypeStruct(observed.shape, F32)] * 2,
        in_specs=[whole] * 8,
        out_specs=[vmem, vmem],
        scratch_shapes=[pltpu.VMEM(operand.shape, operand.dtype) for operand in operands]
        + [
            pltpu.VMEM((NY, SLOTS), BF16),
            pltpu.VMEM((NT, SLOTS), F32),
            pltpu.VMEM((NT, SLOTS), F32),
            pltpu.VMEM((2 * NY, NY), BF16),
            pltpu.VMEM((NY, NY), BF16),
            pltpu.VMEM((NY, NY), BF16),
            pltpu.VMEM((4, NT, 128), F32),
            group_block,
            group_block,
            time_block,
            chip_block,
            chip_block,
            chip_block,
            group_block,
            group_block,
            pltpu.VMEM((GROUP, 32, 128), BF16),
            pltpu.VMEM((GROUP, 32, 128), BF16),
            pltpu.VMEM((8, 4, 16, 128), BF16),
            pltpu.VMEM((CHIPS, 16, 128), BF16),
            pltpu.VMEM((2, 8, 128), F32),
            pltpu.VMEM((CHIPS, 8, 128), F32),
            pltpu.VMEM((GROUP, 8, 128), F32),
            pltpu.SemaphoreType.DMA((8,)),
            pltpu.SemaphoreType.DMA((ITERS, 4)),
            pltpu.SemaphoreType.DMA((ITERS, 4)),
            pltpu.SemaphoreType.DMA((4,)),
            pltpu.SemaphoreType.DMA((4,)),
        ],
        compiler_params=pltpu.CompilerParams(
            collective_id=0, has_side_effects=True, vmem_limit_bytes=63 * 1024 * 1024
        ),
    )(*operands)


def solution(mesh):
    placed = (
        P(None, "gx", "gy", None, None),
        P(None, "gx", "gy", None, None),
        P("gx", "gy", None),
        P("gx", "gy", None, None),
        P("gx", "gy", None, None),
        P(),
        P(),
        P(),
    )
    return jax.shard_map(
        per_device,
        mesh=mesh,
        in_specs=placed,
        out_specs=(P("gx", "gy", None, None), P("gx", "gy", None, None)),
        check_vma=False,
    )
```

```python
import jax
import jax.numpy as jnp
from jax import lax
from jax.experimental import pallas as pl
from jax.experimental.pallas import tpu as pltpu
from jax.sharding import PartitionSpec as P

XS = 4
YS = 64
ITERS = 2
TILES = 4
CAP = 256
SLOTS = TILES * CAP
CHIPS = 32
GROUP = 16
NX = 256
NY = 512
NT = 128
F32 = jnp.float32
BF16 = jnp.bfloat16
MESH = pl.DeviceIdType.MESH
ROW_ROW = (((1,), (1,)), ((), ()))
FAR_X = (2, 1, 3, 0)
FREE = 88


def cubic_weights(fraction):
    square = fraction * fraction
    cubic_term = square * fraction
    return (
        (2.0 * square - cubic_term - fraction) * 0.5,
        (3.0 * cubic_term - 5.0 * square + 2.0) * 0.5,
        (4.0 * square - 3.0 * cubic_term + fraction) * 0.5,
        (cubic_term - square) * 0.5,
    )


def iota(shape, axis):
    return lax.broadcasted_iota(jnp.int32, shape, axis)


def flat(rows):
    return jnp.concatenate([rows[k : k + 1, :] for k in range(TILES)], axis=1)


def dot(left, right):
    return jnp.dot(left, right, preferred_element_type=F32)


def dot_rows(left, right):
    return lax.dot_general(left, right, ROW_ROW, preferred_element_type=F32)


def spread_rows(weights, first, rows):
    total = jnp.zeros(rows.shape, F32)
    for shift in range(4):
        total = total + jnp.where(first + shift == rows, weights[shift], 0.0)
    return total


def third(index):
    return (index * 43) >> 7


def lane_sum(row):
    total = row[:, :128]
    for part in range(1, SLOTS // 128):
        total = total + row[:, 128 * part : 128 * (part + 1)]
    return total


def sum_row(*rows):
    lanes = iota((1, 128), 1)
    total = jnp.zeros((1, 128), F32)
    for k, row in enumerate(rows):
        total = jnp.where(lanes == FREE + k, jnp.sum(row, axis=1, keepdims=True), total)
    return total


def totals_of(row, count):
    return [
        jnp.sum(jnp.where(iota(row.shape, 1) == FREE + k, row, 0.0), axis=1, keepdims=True)
        for k in range(count)
    ]


def pieces(row):
    high = row.astype(BF16).astype(F32)
    middle = (row - high).astype(BF16).astype(F32)
    return high, middle, (row - high - middle).astype(BF16).astype(F32)


def group_tile(row):
    rows = iota((8, 128), 0)
    tile = jnp.zeros((8, 128), F32)
    for k, piece in enumerate(pieces(row)):
        tile = jnp.where(rows == k, piece, tile)
    return tile


def chip_tile(row):
    high, middle, low = pieces(row)
    rows = iota((16, 128), 0)
    tile = jnp.where(rows == 7, high + pltpu.roll(low, 8, 1), 0.0)
    return jnp.where(rows == 15, middle, tile)


def group_rows(received):
    rows = []
    for member in range(GROUP):
        tile = received[member, 16:, :].astype(F32)
        rows.append(tile[8:9, :] + tile[9:10, :] + tile[10:11, :])
    return jnp.concatenate(rows, axis=0)


def chip_rows(received):
    rows = []
    for chip in range(CHIPS):
        tile = received[chip].astype(F32)
        rows.append(tile[7:8, :] + tile[15:16, :] + pltpu.roll(tile[7:8, :], 120, 1))
    return jnp.concatenate(rows, axis=0)


def quotient(above, below):
    return jnp.where(below > 0.0, above / jnp.where(below > 0.0, below, 1.0), 0.0)


def kernel(
    cells_hbm,
    offsets_hbm,
    counts_hbm,
    observed_hbm,
    noise_hbm,
    kx_hbm,
    ky_hbm,
    kt_hbm,
    result_ref,
    cells_ref,
    offsets_ref,
    counts_ref,
    observed_ref,
    noise_ref,
    kx_ref,
    ky_ref,
    kt_ref,
    plane,
    time_rows,
    mixed_rows,
    mix_y,
    mix_x,
    select,
    turn,
    send_a,
    recv_a,
    send_b,
    recv_b,
    send_c,
    recv_c,
    send_d,
    recv_d,
    send_ga,
    recv_ga,
    send_gb,
    recv_gb,
    sums_sent,
    sums_chips,
    sums_group,
    load_sem,
    send_sem,
    recv_sem,
    plain_sem,
    sum_sem,
):
    block_x = lax.axis_index("gx")
    block_y = lax.axis_index("gy")
    chip = block_x // 2
    core = block_x % 2
    chip_x = chip // 8
    chip_y = chip % 8
    member = block_y * 2 + core

    def far(step):
        return 4 + (step // 2) * (1 - step % 2) - ((step + 1) // 2) * (step % 2)

    def each_of_group(act):
        def one(step, carry):
            z = (block_y + far(step)) % 8
            act(z * 2 + 1 - core, (chip * 2 + 1 - core, z))
            return carry

        def same(step, carry):
            z = (block_y + far(step)) % 8
            act(z * 2 + core, (chip * 2 + core, z))
            return carry

        lax.fori_loop(0, 7, one, 0)
        lax.fori_loop(0, 7, same, 0)
        act(block_y * 2 + 1 - core, (chip * 2 + 1 - core, block_y))

    def each_of_chips(act):
        def one(step, carry):
            y = (chip_y + far(step)) % 8
            for shift in FAR_X:
                place = (chip_x + shift) % 4 * 8 + y
                act(place, (place * 2 + core, block_y))
            return carry

        lax.fori_loop(0, 7, one, 0)
        for shift in FAR_X[:3]:
            place = (chip_x + shift) % 4 * 8 + chip_y
            act(place, (place * 2 + core, block_y))

    barrier = pltpu.get_barrier_semaphore()

    def greet(place, device):
        pl.semaphore_signal(barrier, inc=1, device_id=device, device_id_type=MESH)

    each_of_chips(greet)
    loads = [
        pltpu.make_async_copy(source, target, load_sem.at[k])
        for k, (source, target) in enumerate(
            (
                (cells_hbm, cells_ref),
                (offsets_hbm, offsets_ref),
                (counts_hbm, counts_ref),
                (observed_hbm, observed_ref),
                (noise_hbm, noise_ref),
                (kt_hbm, kt_ref),
                (ky_hbm, ky_ref),
                (kx_hbm, kx_ref),
            )
        )
    ]
    for load in loads:
        load.start()
    each_of_group(greet)
    for load in loads[:6]:
        load.wait()

    live = jnp.concatenate(
        [
            (iota((1, CAP), 1) < counts_ref[0, :, k : k + 1]).astype(F32)
            for k in range(TILES)
        ],
        axis=1,
    )
    noise = flat(noise_ref[0, 0])
    start = live * flat(observed_ref[0, 0])
    weights_x = cubic_weights(flat(offsets_ref[0, 0, 0]))
    weights_y = cubic_weights(flat(offsets_ref[1, 0, 0]))
    weights_t = cubic_weights(flat(offsets_ref[2, 0, 0]))
    first_x = flat(cells_ref[0, 0, 0]) - XS * block_x
    first_y = flat(cells_ref[1, 0, 0]) - YS * block_y
    first_t = flat(cells_ref[2, 0, 0]) - 1
    rows_y = spread_rows(weights_y, first_y, iota((YS, SLOTS), 0) + 1)
    for x in range(7):
        row_x = spread_rows(weights_x, first_x, jnp.full((1, SLOTS), x, jnp.int32))
        plane[x * YS : (x + 1) * YS, :] = (row_x * rows_y).astype(BF16)
    edge_row = iota((YS, SLOTS), 0)
    edge_x = third(edge_row)
    edge_y = edge_row - 3 * edge_x
    edge_y = jnp.where(edge_y == 0, 0, YS + edge_y)
    plane[7 * YS :, :] = (
        spread_rows(weights_x, first_x, edge_x) * spread_rows(weights_y, first_y, edge_y)
    ).astype(BF16)
    rows_t = spread_rows(weights_t, first_t, iota((NT, SLOTS), 0)) * live
    time_rows[...] = rows_t
    high = rows_t.astype(BF16)
    low = (rows_t - high.astype(F32)).astype(BF16)
    kt = kt_ref[...]
    mixed_rows[...] = dot(kt, high) + dot(kt, low)

    low_half = iota((32, 128), 1) < 64
    edge_lane = third(iota((8, NY), 1) & 63)

    def wait_bytes(ref, count, semaphore):
        block = ref.at[pl.ds(0, count)]
        pltpu.make_async_copy(block, block, semaphore).wait()

    def copy_group(source, target, sent, received):
        def act(place, device):
            pltpu.make_async_remote_copy(
                src_ref=source(place),
                dst_ref=target.at[member],
                send_sem=sent,
                recv_sem=received,
                device_id=device,
                device_id_type=MESH,
            ).start()

        each_of_group(act)

    def copy_chips(source, target, sent, received):
        def act(place, device):
            pltpu.make_async_remote_copy(
                src_ref=source(place),
                dst_ref=target.at[chip],
                send_sem=sent,
                recv_sem=received,
                device_id=device,
                device_id_type=MESH,
            ).start()

        each_of_chips(act)

    def time_blocks(spread, tile):
        blocks = [
            spread[:, 128 * pair : 128 * (pair + 1)].reshape(GROUP, 8, 128) for pair in range(4)
        ]
        if tile is not None:
            blocks[3] = blocks[3] + tile[None]
        return jnp.concatenate(blocks, axis=1).astype(BF16)

    def whole_rows(received):
        columns = []
        for pair in range(4):
            parts = []
            for half in range(2):
                lower = received[4 * pair + half]
                upper = received[4 * pair + 2 + half]
                parts.append(jnp.where(low_half, lower, pltpu.roll(upper, 64, 1)))
                parts.append(jnp.where(low_half, pltpu.roll(lower, 64, 1), upper))
            columns.append(jnp.concatenate(parts, axis=0))
        main = jnp.concatenate(columns, axis=1)
        zero = jnp.zeros((8, NY), F32)
        main_parts, edge_parts = [], []
        for half in range(2):
            edge = main[64 * half + 56 : 64 * half + 64, :]
            main_parts.append(main[64 * half : 64 * half + 56, :])
            main_parts.append(zero)
            for row in range(7):
                x = 2 * (row % 4) + row // 4
                edge_parts.append(jnp.where(edge_lane == x, edge, 0.0))
            edge_parts.append(zero)
        return jnp.concatenate(main_parts, axis=0), jnp.concatenate(edge_parts, axis=0)

    def to_column_blocks(rows, target, tile):
        for row in range(16):
            for quarter in range(4):
                turn[quarter, pl.ds(row, 8, stride=16), :] = rows[
                    8 * row : 8 * row + 8, 128 * quarter : 128 * (quarter + 1)
                ]
        for quarter in range(4):
            blocks = turn[quarter].reshape(8, 16, 128)
            if tile is not None:
                blocks = blocks + tile[None]
            target[:, quarter] = blocks.astype(BF16)

    def spread_out(turn_index, vector, tile):
        weighted = (mixed_rows[...] * vector).astype(BF16)
        send_a[turn_index] = time_blocks(dot_rows(weighted, plane[...]), tile)
        if turn_index == 0:
            pl.semaphore_wait(barrier, GROUP - 1 + CHIPS - 1)
        copy_group(
            lambda place: send_a.at[turn_index, place],
            recv_a.at[turn_index],
            send_sem.at[turn_index, 0],
            recv_sem.at[turn_index, 0],
        )
        recv_a[turn_index, member] = send_a[turn_index, member]

    def spread_plain(vector):
        weighted = (time_rows[...] * vector).astype(BF16)
        send_ga[...] = time_blocks(dot_rows(weighted, plane[...]), None)
        copy_group(lambda place: send_ga.at[place], recv_ga, plain_sem.at[0], plain_sem.at[1])
        recv_ga[member] = send_ga[member]

    def arrived_blocks(turn_index):
        wait_bytes(recv_a.at[turn_index], GROUP - 1, recv_sem.at[turn_index, 0])
        return [recv_a[turn_index, place].astype(F32) for place in range(GROUP)]

    def mix_along_y(turn_index, blocks, tile):
        main, edge = whole_rows(blocks)
        left = jnp.concatenate([main, edge], axis=1).astype(BF16)
        to_column_blocks(dot(left, mix_y[...]), send_b.at[turn_index], tile)
        copy_chips(
            lambda place: send_b.at[turn_index, place // 4, place % 4],
            recv_b.at[turn_index],
            send_sem.at[turn_index, 1],
            recv_sem.at[turn_index, 1],
        )
        recv_b[turn_index, chip] = send_b[turn_index, chip // 4, chip % 4]

    def fold_plain():
        wait_bytes(recv_ga, GROUP - 1, plain_sem.at[1])
        main, edge = whole_rows([recv_ga[place].astype(F32) for place in range(GROUP)])
        to_column_blocks(main + dot(edge.astype(BF16), select[...]), send_gb, None)
        copy_chips(
            lambda place: send_gb.at[place // 4, place % 4],
            recv_gb,
            plain_sem.at[2],
            plain_sem.at[3],
        )
        recv_gb[chip] = send_gb[chip // 4, chip % 4]

    def grid_columns(turn_index):
        wait_bytes(recv_b.at[turn_index], CHIPS - 1, recv_sem.at[turn_index, 1])
        return recv_b[turn_index].reshape(NY, 128)

    def spread_columns():
        wait_bytes(recv_gb, CHIPS - 1, plain_sem.at[3])
        return recv_gb[...].reshape(NY, 128).astype(F32)

    def send_field(turn_index, field):
        send_c[turn_index] = field.astype(BF16).reshape(CHIPS, 16, 128)
        copy_chips(
            lambda place: send_c.at[turn_index, place],
            recv_c.at[turn_index],
            send_sem.at[turn_index, 2],
            recv_sem.at[turn_index, 2],
        )
        recv_c[turn_index, chip] = send_c[turn_index, chip]

    def field_back(turn_index):
        wait_bytes(recv_c.at[turn_index], CHIPS - 1, recv_sem.at[turn_index, 2])
        for time in range(8):
            for quarter in range(4):
                turn[quarter, 16 * time : 16 * time + 16, :] = recv_c[
                    turn_index, 4 * time + quarter
                ].astype(F32)
        rows = [
            jnp.concatenate(
                [turn[quarter, pl.ds(row, 8, stride=16), :] for quarter in range(4)], axis=1
            )
            for row in range(16)
        ]
        edges = dot_rows(jnp.concatenate(rows, axis=0).astype(BF16), select[...])
        for half in range(2):
            edge = jnp.zeros((8, NY), F32)
            for row in range(7):
                x = 2 * (row % 4) + row // 4
                first = 64 * half + 8 * row
                edge = edge + jnp.where(edge_lane == x, edges[first : first + 8, :], 0.0)
            even = jnp.concatenate(rows[8 * half : 8 * half + 4], axis=0)
            odd = jnp.concatenate(rows[8 * half + 4 : 8 * half + 7] + [edge], axis=0)
            for pair in range(4):
                lanes = slice(128 * pair, 128 * (pair + 1))
                lower = jnp.where(low_half, even[:, lanes], pltpu.roll(odd[:, lanes], 64, 1))
                upper = jnp.where(low_half, pltpu.roll(even[:, lanes], 64, 1), odd[:, lanes])
                send_d[turn_index, 4 * pair + half] = lower.astype(BF16)
                send_d[turn_index, 4 * pair + 2 + half] = upper.astype(BF16)
        copy_group(
            lambda place: send_d.at[turn_index, place],
            recv_d.at[turn_index],
            send_sem.at[turn_index, 3],
            recv_sem.at[turn_index, 3],
        )
        recv_d[turn_index, member] = send_d[turn_index, member]

    def at_slots(turn_index):
        wait_bytes(recv_d.at[turn_index], GROUP - 1, recv_sem.at[turn_index, 3])
        arrived = recv_d[turn_index].astype(F32)
        around = jnp.concatenate(
            [arrived[:, 8 * pair : 8 * pair + 8, :].reshape(NT, 128) for pair in range(4)], axis=1
        ).astype(BF16)
        picked = dot(around, plane[...])
        return jnp.sum(picked * time_rows[...], axis=0, keepdims=True)

    spread_out(0, start, None)

    for load in loads[6:]:
        load.wait()
    edge_index = iota((NY, NY), 0)
    slot = edge_index & 63
    slot_x = third(slot)
    slot_y = slot - 3 * slot_x
    cell_y = (edge_index >> 6) * YS + jnp.where(slot_y == 0, -1, YS - 1 + slot_y)
    cell_y = jnp.where(slot < 21, cell_y, -1)
    select[...] = (cell_y == iota((NY, NY), 1)).astype(F32).astype(BF16)
    ky = ky_ref[...]
    mix_y[:NY, :] = ky
    mix_y[NY:, :] = dot(select[...], ky).astype(BF16)
    wide_row = iota((NY, NX), 0)
    wide_x = 2 * (wide_row & 3) + ((wide_row >> 2) & 1)
    cell_x = (wide_row >> 3) * XS - 1 + wide_x
    cell_x = jnp.where(wide_x < 7, cell_x, -1)
    widen = (cell_x == iota((NY, NX), 1)).astype(F32).astype(BF16)
    mix_x[...] = dot_rows(dot(widen, kx_ref[...]).astype(BF16), widen).astype(BF16)

    mix_along_y(0, arrived_blocks(0), None)
    send_field(0, dot(mix_x[...], grid_columns(0)))
    field_back(0)
    image_0 = at_slots(0) + noise * start

    sums = sum_row(
        lane_sum(start * start),
        lane_sum(start * image_0),
        lane_sum(image_0 * image_0),
        lane_sum(noise * start * image_0),
        lane_sum(noise * image_0 * image_0),
    )
    own = totals_of(sums, 2)
    spread_out(1, image_0 - quotient(own[1], own[0]) * start, group_tile(sums))
    spread_plain(image_0)
    blocks = arrived_blocks(1)
    member_sums = group_rows(recv_a[1])
    group_sums = jnp.sum(member_sums, axis=0, keepdims=True)
    members = totals_of(member_sums, 2)
    group = totals_of(group_sums, 2)
    part = quotient(members[1], members[0]) - quotient(group[1], group[0])
    blocks = [
        blocks[place] + part[place : place + 1, :] * recv_a[0, place].astype(F32)
        for place in range(GROUP)
    ]
    mix_along_y(1, blocks, chip_tile(group_sums))
    fold_plain()
    grid_columns(1)
    chip_sums = chip_rows(recv_b[1])
    chips = totals_of(chip_sums, 2)
    rr, along, square, noise_01, noise_11 = totals_of(
        jnp.sum(chip_sums, axis=0, keepdims=True), 5
    )
    step_0 = rr / along
    grow = step_0 * (square / along)
    ratio = jnp.maximum(grow - 1.0, 0.0)
    new = rr * ratio
    part = grow - step_0 * quotient(chips[1], chips[0])
    columns = jnp.concatenate(
        [
            part[place : place + 1, :] * recv_b[0, place].astype(F32)
            - step_0 * recv_b[1, place].astype(F32)
            for place in range(CHIPS)
        ],
        axis=0,
    )
    field = dot(mix_x[...], columns.astype(BF16))
    send_field(1, field)
    inner = jnp.sum(jnp.sum(field * spread_columns(), axis=0, keepdims=True), axis=1, keepdims=True)
    inner = jnp.broadcast_to(inner, (8, 128))
    sums_sent[0] = inner
    sums_group[member] = inner
    copy_group(lambda place: sums_sent.at[0], sums_group, sum_sem.at[2], sum_sem.at[3])
    field_back(1)
    wait_bytes(sums_group, GROUP - 1, sum_sem.at[3])
    inner = jnp.sum(sums_group[...], axis=0)
    sums_sent[1] = inner
    sums_chips[chip] = inner
    copy_chips(lambda place: sums_sent.at[1], sums_chips, sum_sem.at[0], sum_sem.at[1])
    direction = grow * start - step_0 * image_0
    image_1 = at_slots(1) + noise * direction
    wait_bytes(sums_chips, CHIPS - 1, sum_sem.at[1])
    inner = jnp.sum(sums_chips[...], axis=0)[:1, :1]
    curvature = -step_0 * (inner + grow * noise_01 - step_0 * noise_11)
    step_1 = new / curvature
    solved = step_0 * start + step_1 * direction
    rest = start - step_0 * image_0 - step_1 * image_1
    for k in range(TILES):
        result_ref[0, 0, 0, k : k + 1, :] = solved[:, CAP * k : CAP * (k + 1)]
        result_ref[1, 0, 0, k : k + 1, :] = rest[:, CAP * k : CAP * (k + 1)]

    for turn_index in range(ITERS):
        wait_bytes(recv_a.at[turn_index], GROUP - 1, send_sem.at[turn_index, 0])
        wait_bytes(recv_b.at[turn_index], CHIPS - 1, send_sem.at[turn_index, 1])
        wait_bytes(recv_c.at[turn_index], CHIPS - 1, send_sem.at[turn_index, 2])
        wait_bytes(recv_d.at[turn_index], GROUP - 1, send_sem.at[turn_index, 3])
    wait_bytes(recv_ga, GROUP - 1, plain_sem.at[0])
    wait_bytes(recv_gb, CHIPS - 1, plain_sem.at[2])
    wait_bytes(sums_chips, CHIPS - 1, sum_sem.at[0])
    wait_bytes(sums_group, GROUP - 1, sum_sem.at[2])


def per_device(cells, offsets, counts, observed, noise, kernel_x, kernel_y, kernel_t):
    vmem = pl.BlockSpec(memory_space=pltpu.VMEM)
    whole = pl.BlockSpec(memory_space=pltpu.HBM)
    group_block = pltpu.VMEM((ITERS, GROUP, 32, 128), BF16)
    chip_block = pltpu.VMEM((ITERS, CHIPS, 16, 128), BF16)
    time_block = pltpu.VMEM((ITERS, 8, 4, 16, 128), BF16)
    operands = (cells, offsets, counts, observed, noise, kernel_x, kernel_y, kernel_t)
    result = pl.pallas_call(
        kernel,
        out_shape=jax.ShapeDtypeStruct((2, *observed.shape), F32),
        in_specs=[whole] * 8,
        out_specs=vmem,
        scratch_shapes=[pltpu.VMEM(operand.shape, operand.dtype) for operand in operands]
        + [
            pltpu.VMEM((NY, SLOTS), BF16),
            pltpu.VMEM((NT, SLOTS), F32),
            pltpu.VMEM((NT, SLOTS), F32),
            pltpu.VMEM((2 * NY, NY), BF16),
            pltpu.VMEM((NY, NY), BF16),
            pltpu.VMEM((NY, NY), BF16),
            pltpu.VMEM((4, NT, 128), F32),
            group_block,
            group_block,
            time_block,
            chip_block,
            chip_block,
            chip_block,
            group_block,
            group_block,
            pltpu.VMEM((GROUP, 32, 128), BF16),
            pltpu.VMEM((GROUP, 32, 128), BF16),
            pltpu.VMEM((8, 4, 16, 128), BF16),
            pltpu.VMEM((CHIPS, 16, 128), BF16),
            pltpu.VMEM((2, 8, 128), F32),
            pltpu.VMEM((CHIPS, 8, 128), F32),
            pltpu.VMEM((GROUP, 8, 128), F32),
            pltpu.SemaphoreType.DMA((8,)),
            pltpu.SemaphoreType.DMA((ITERS, 4)),
            pltpu.SemaphoreType.DMA((ITERS, 4)),
            pltpu.SemaphoreType.DMA((4,)),
            pltpu.SemaphoreType.DMA((4,)),
        ],
        compiler_params=pltpu.CompilerParams(
            collective_id=0, has_side_effects=True, vmem_limit_bytes=63 * 1024 * 1024
        ),
    )(*operands)
    return result[0], result[1]


def solution(mesh):
    placed = (
        P(None, "gx", "gy", None, None),
        P(None, "gx", "gy", None, None),
        P("gx", "gy", None),
        P("gx", "gy", None, None),
        P("gx", "gy", None, None),
        P(),
        P(),
        P(),
    )
    return jax.shard_map(
        per_device,
        mesh=mesh,
        in_specs=placed,
        out_specs=(P("gx", "gy", None, None), P("gx", "gy", None, None)),
        check_vma=False,
    )
```

```python
import jax
import jax.numpy as jnp
from jax import lax
from jax.experimental import pallas as pl
from jax.experimental.pallas import tpu as pltpu
from jax.sharding import PartitionSpec as P

XS = 4
YS = 64
ITERS = 2
TILES = 4
CAP = 256
SLOTS = TILES * CAP
CHIPS = 32
GROUP = 16
NX = 256
NY = 512
NT = 128
F32 = jnp.float32
BF16 = jnp.bfloat16
MESH = pl.DeviceIdType.MESH
ROW_ROW = (((1,), (1,)), ((), ()))
FAR_X = (2, 1, 3, 0)
FREE = 88


def cubic_weights(fraction):
    square = fraction * fraction
    cubic_term = square * fraction
    return (
        (2.0 * square - cubic_term - fraction) * 0.5,
        (3.0 * cubic_term - 5.0 * square + 2.0) * 0.5,
        (4.0 * square - 3.0 * cubic_term + fraction) * 0.5,
        (cubic_term - square) * 0.5,
    )


def iota(shape, axis):
    return lax.broadcasted_iota(jnp.int32, shape, axis)


def flat(rows):
    return jnp.concatenate([rows[k : k + 1, :] for k in range(TILES)], axis=1)


def dot(left, right):
    return jnp.dot(left, right, preferred_element_type=F32)


def dot_rows(left, right):
    return lax.dot_general(left, right, ROW_ROW, preferred_element_type=F32)


def spread_rows(weights, first, rows):
    total = jnp.zeros(rows.shape, F32)
    for shift in range(4):
        total = total + jnp.where(first + shift == rows, weights[shift], 0.0)
    return total


def third(index):
    return (index * 43) >> 7


def lane_sum(row):
    total = row[:, :128]
    for part in range(1, SLOTS // 128):
        total = total + row[:, 128 * part : 128 * (part + 1)]
    return total


def sum_row(*rows):
    lanes = iota((1, 128), 1)
    total = jnp.zeros((1, 128), F32)
    for k, row in enumerate(rows):
        total = jnp.where(lanes == FREE + k, jnp.sum(row, axis=1, keepdims=True), total)
    return total


def totals_of(row, count):
    return [
        jnp.sum(jnp.where(iota(row.shape, 1) == FREE + k, row, 0.0), axis=1, keepdims=True)
        for k in range(count)
    ]


def pieces(row):
    high = row.astype(BF16).astype(F32)
    middle = (row - high).astype(BF16).astype(F32)
    return high, middle, (row - high - middle).astype(BF16).astype(F32)


def group_tile(row):
    rows = iota((8, 128), 0)
    tile = jnp.zeros((8, 128), F32)
    for k, piece in enumerate(pieces(row)):
        tile = jnp.where(rows == k, piece, tile)
    return tile


def chip_tile(row):
    high, middle, low = pieces(row)
    rows = iota((16, 128), 0)
    tile = jnp.where(rows == 7, high + pltpu.roll(low, 8, 1), 0.0)
    return jnp.where(rows == 15, middle, tile)


def group_rows(received):
    rows = []
    for member in range(GROUP):
        tile = received[member, 16:, :].astype(F32)
        rows.append(tile[8:9, :] + tile[9:10, :] + tile[10:11, :])
    return jnp.concatenate(rows, axis=0)


def chip_rows(received):
    rows = []
    for chip in range(CHIPS):
        tile = received[chip].astype(F32)
        rows.append(tile[7:8, :] + tile[15:16, :] + pltpu.roll(tile[7:8, :], 120, 1))
    return jnp.concatenate(rows, axis=0)


def quotient(above, below):
    return jnp.where(below > 0.0, above / jnp.where(below > 0.0, below, 1.0), 0.0)


def kernel(
    cells_hbm,
    offsets_hbm,
    counts_hbm,
    observed_hbm,
    noise_hbm,
    kx_hbm,
    ky_hbm,
    kt_hbm,
    result_ref,
    cells_ref,
    offsets_ref,
    counts_ref,
    observed_ref,
    noise_ref,
    kx_ref,
    ky_ref,
    kt_ref,
    plane,
    time_rows,
    mixed_rows,
    mix_y,
    mix_x,
    select,
    turn,
    send_a,
    recv_a,
    send_b,
    recv_b,
    send_c,
    recv_c,
    send_d,
    recv_d,
    send_ga,
    recv_ga,
    send_gb,
    recv_gb,
    sums_sent,
    sums_chips,
    sums_group,
    load_sem,
    send_sem,
    recv_sem,
    plain_sem,
    sum_sem,
    entered,
):
    block_x = lax.axis_index("gx")
    block_y = lax.axis_index("gy")
    chip = block_x // 2
    core = block_x % 2
    chip_x = chip // 8
    chip_y = chip % 8
    member = block_y * 2 + core

    def far(step):
        return 4 + (step // 2) * (1 - step % 2) - ((step + 1) // 2) * (step % 2)

    def each_of_group(act):
        def one(step, carry):
            z = (block_y + far(step)) % 8
            act(z * 2 + 1 - core, (chip * 2 + 1 - core, z))
            return carry

        def same(step, carry):
            z = (block_y + far(step)) % 8
            act(z * 2 + core, (chip * 2 + core, z))
            return carry

        lax.fori_loop(0, 7, one, 0)
        lax.fori_loop(0, 7, same, 0)
        act(block_y * 2 + 1 - core, (chip * 2 + 1 - core, block_y))

    def each_of_chips(act):
        def one(step, carry):
            y = (chip_y + far(step)) % 8
            for shift in FAR_X:
                place = (chip_x + shift) % 4 * 8 + y
                act(place, (place * 2 + core, block_y))
            return carry

        lax.fori_loop(0, 7, one, 0)
        for shift in FAR_X[:3]:
            place = (chip_x + shift) % 4 * 8 + chip_y
            act(place, (place * 2 + core, block_y))

    barrier = pltpu.get_barrier_semaphore()

    def greet(place, device):
        pl.semaphore_signal(barrier, inc=1, device_id=device, device_id_type=MESH)

    def greet_row(act):
        for shift in FAR_X[:3]:
            place = (chip_x + shift) % 4 * 8 + chip_y
            act(place, (place * 2 + core, block_y))

    def greet_column(act):
        def one(step, carry):
            place = chip_x * 8 + (chip_y + far(step)) % 8
            act(place, (place * 2 + core, block_y))
            return carry

        lax.fori_loop(0, 7, one, 0)

    def greet_again(place, device):
        pl.semaphore_signal(entered, inc=1, device_id=device, device_id_type=MESH)

    for step in (4, 3, 5, 2, 6, 1, 7):
        for other in (0, 1):
            z = (block_y + step) % 8
            greet(None, (chip * 2 + other, z))
    greet(None, (chip * 2 + 1 - core, block_y))
    for step in (4, 3, 5, 2, 6, 1, 7):
        place = chip_x * 8 + (chip_y + step) % 8
        greet(None, (place * 2 + core, block_y))
    greet_row(greet)
    loads = [
        pltpu.make_async_copy(source, target, load_sem.at[k])
        for k, (source, target) in enumerate(
            (
                (cells_hbm, cells_ref),
                (offsets_hbm, offsets_ref),
                (counts_hbm, counts_ref),
                (observed_hbm, observed_ref),
                (noise_hbm, noise_ref),
                (kt_hbm, kt_ref),
                (ky_hbm, ky_ref),
                (kx_hbm, kx_ref),
            )
        )
    ]
    for load in loads:
        load.start()
    for load in loads[:6]:
        load.wait()

    live = jnp.concatenate(
        [
            (iota((1, CAP), 1) < counts_ref[0, :, k : k + 1]).astype(F32)
            for k in range(TILES)
        ],
        axis=1,
    )
    noise = flat(noise_ref[0, 0])
    start = live * flat(observed_ref[0, 0])
    weights_x = cubic_weights(flat(offsets_ref[0, 0, 0]))
    weights_y = cubic_weights(flat(offsets_ref[1, 0, 0]))
    weights_t = cubic_weights(flat(offsets_ref[2, 0, 0]))
    first_x = flat(cells_ref[0, 0, 0]) - XS * block_x
    first_y = flat(cells_ref[1, 0, 0]) - YS * block_y
    first_t = flat(cells_ref[2, 0, 0]) - 1
    rows_y = spread_rows(weights_y, first_y, iota((YS, SLOTS), 0) + 1)
    for x in range(7):
        row_x = spread_rows(weights_x, first_x, jnp.full((1, SLOTS), x, jnp.int32))
        plane[x * YS : (x + 1) * YS, :] = (row_x * rows_y).astype(BF16)
    edge_row = iota((YS, SLOTS), 0)
    edge_x = third(edge_row)
    edge_y = edge_row - 3 * edge_x
    edge_y = jnp.where(edge_y == 0, 0, YS + edge_y)
    plane[7 * YS :, :] = (
        spread_rows(weights_x, first_x, edge_x) * spread_rows(weights_y, first_y, edge_y)
    ).astype(BF16)
    rows_t = spread_rows(weights_t, first_t, iota((NT, SLOTS), 0)) * live
    time_rows[...] = rows_t
    high = rows_t.astype(BF16)
    low = (rows_t - high.astype(F32)).astype(BF16)
    kt = kt_ref[...]
    mixed_rows[...] = dot(kt, high) + dot(kt, low)

    low_half = iota((32, 128), 1) < 64
    edge_lane = third(iota((8, NY), 1) & 63)

    def wait_bytes(ref, count, semaphore):
        block = ref.at[pl.ds(0, count)]
        pltpu.make_async_copy(block, block, semaphore).wait()

    def copy_group(source, target, sent, received):
        def act(place, device):
            pltpu.make_async_remote_copy(
                src_ref=source(place),
                dst_ref=target.at[member],
                send_sem=sent,
                recv_sem=received,
                device_id=device,
                device_id_type=MESH,
            ).start()

        each_of_group(act)

    def copy_chips(source, target, sent, received):
        def act(place, device):
            pltpu.make_async_remote_copy(
                src_ref=source(place),
                dst_ref=target.at[chip],
                send_sem=sent,
                recv_sem=received,
                device_id=device,
                device_id_type=MESH,
            ).start()

        each_of_chips(act)

    def time_blocks(spread, tile):
        blocks = [
            spread[:, 128 * pair : 128 * (pair + 1)].reshape(GROUP, 8, 128) for pair in range(4)
        ]
        if tile is not None:
            blocks[3] = blocks[3] + tile[None]
        return jnp.concatenate(blocks, axis=1).astype(BF16)

    def whole_rows(received):
        columns = []
        for pair in range(4):
            parts = []
            for half in range(2):
                lower = received[4 * pair + half]
                upper = received[4 * pair + 2 + half]
                parts.append(jnp.where(low_half, lower, pltpu.roll(upper, 64, 1)))
                parts.append(jnp.where(low_half, pltpu.roll(lower, 64, 1), upper))
            columns.append(jnp.concatenate(parts, axis=0))
        main = jnp.concatenate(columns, axis=1)
        zero = jnp.zeros((8, NY), F32)
        main_parts, edge_parts = [], []
        for half in range(2):
            edge = main[64 * half + 56 : 64 * half + 64, :]
            main_parts.append(main[64 * half : 64 * half + 56, :])
            main_parts.append(zero)
            for row in range(7):
                x = 2 * (row % 4) + row // 4
                edge_parts.append(jnp.where(edge_lane == x, edge, 0.0))
            edge_parts.append(zero)
        return jnp.concatenate(main_parts, axis=0), jnp.concatenate(edge_parts, axis=0)

    def to_column_blocks(rows, target, tile):
        for row in range(16):
            for quarter in range(4):
                turn[quarter, pl.ds(row, 8, stride=16), :] = rows[
                    8 * row : 8 * row + 8, 128 * quarter : 128 * (quarter + 1)
                ]
        for quarter in range(4):
            blocks = turn[quarter].reshape(8, 16, 128)
            if tile is not None:
                blocks = blocks + tile[None]
            target[:, quarter] = blocks.astype(BF16)

    def spread_out(turn_index, vector, tile):
        weighted = (mixed_rows[...] * vector).astype(BF16)
        send_a[turn_index] = time_blocks(dot_rows(weighted, plane[...]), tile)
        if turn_index == 0:
            pl.semaphore_wait(barrier, GROUP - 1 + 7 + 3)
        copy_group(
            lambda place: send_a.at[turn_index, place],
            recv_a.at[turn_index],
            send_sem.at[turn_index, 0],
            recv_sem.at[turn_index, 0],
        )
        if turn_index == 0:
            greet_row(greet_again)
        recv_a[turn_index, member] = send_a[turn_index, member]

    def spread_plain(vector):
        weighted = (time_rows[...] * vector).astype(BF16)
        send_ga[...] = time_blocks(dot_rows(weighted, plane[...]), None)
        copy_group(lambda place: send_ga.at[place], recv_ga, plain_sem.at[0], plain_sem.at[1])
        recv_ga[member] = send_ga[member]

    def arrived_blocks(turn_index):
        wait_bytes(recv_a.at[turn_index], GROUP - 1, recv_sem.at[turn_index, 0])
        return [recv_a[turn_index, place].astype(F32) for place in range(GROUP)]

    def mix_along_y(turn_index, blocks, tile):
        main, edge = whole_rows(blocks)
        left = jnp.concatenate([main, edge], axis=1).astype(BF16)
        to_column_blocks(dot(left, mix_y[...]), send_b.at[turn_index], tile)
        if turn_index == 0:
            pl.semaphore_wait(entered, 3)
        copy_chips(
            lambda place: send_b.at[turn_index, place // 4, place % 4],
            recv_b.at[turn_index],
            send_sem.at[turn_index, 1],
            recv_sem.at[turn_index, 1],
        )
        recv_b[turn_index, chip] = send_b[turn_index, chip // 4, chip % 4]

    def fold_plain():
        wait_bytes(recv_ga, GROUP - 1, plain_sem.at[1])
        main, edge = whole_rows([recv_ga[place].astype(F32) for place in range(GROUP)])
        to_column_blocks(main + dot(edge.astype(BF16), select[...]), send_gb, None)
        copy_chips(
            lambda place: send_gb.at[place // 4, place % 4],
            recv_gb,
            plain_sem.at[2],
            plain_sem.at[3],
        )
        recv_gb[chip] = send_gb[chip // 4, chip % 4]

    def grid_columns(turn_index):
        wait_bytes(recv_b.at[turn_index], CHIPS - 1, recv_sem.at[turn_index, 1])
        return recv_b[turn_index].reshape(NY, 128)

    def spread_columns():
        wait_bytes(recv_gb, CHIPS - 1, plain_sem.at[3])
        return recv_gb[...].reshape(NY, 128).astype(F32)

    def send_field(turn_index, field):
        send_c[turn_index] = field.astype(BF16).reshape(CHIPS, 16, 128)
        copy_chips(
            lambda place: send_c.at[turn_index, place],
            recv_c.at[turn_index],
            send_sem.at[turn_index, 2],
            recv_sem.at[turn_index, 2],
        )
        recv_c[turn_index, chip] = send_c[turn_index, chip]

    def field_back(turn_index):
        wait_bytes(recv_c.at[turn_index], CHIPS - 1, recv_sem.at[turn_index, 2])
        for time in range(8):
            for quarter in range(4):
                turn[quarter, 16 * time : 16 * time + 16, :] = recv_c[
                    turn_index, 4 * time + quarter
                ].astype(F32)
        rows = [
            jnp.concatenate(
                [turn[quarter, pl.ds(row, 8, stride=16), :] for quarter in range(4)], axis=1
            )
            for row in range(16)
        ]
        edges = dot_rows(jnp.concatenate(rows, axis=0).astype(BF16), select[...])
        for half in range(2):
            edge = jnp.zeros((8, NY), F32)
            for row in range(7):
                x = 2 * (row % 4) + row // 4
                first = 64 * half + 8 * row
                edge = edge + jnp.where(edge_lane == x, edges[first : first + 8, :], 0.0)
            even = jnp.concatenate(rows[8 * half : 8 * half + 4], axis=0)
            odd = jnp.concatenate(rows[8 * half + 4 : 8 * half + 7] + [edge], axis=0)
            for pair in range(4):
                lanes = slice(128 * pair, 128 * (pair + 1))
                lower = jnp.where(low_half, even[:, lanes], pltpu.roll(odd[:, lanes], 64, 1))
                upper = jnp.where(low_half, pltpu.roll(even[:, lanes], 64, 1), odd[:, lanes])
                send_d[turn_index, 4 * pair + half] = lower.astype(BF16)
                send_d[turn_index, 4 * pair + 2 + half] = upper.astype(BF16)
        copy_group(
            lambda place: send_d.at[turn_index, place],
            recv_d.at[turn_index],
            send_sem.at[turn_index, 3],
            recv_sem.at[turn_index, 3],
        )
        recv_d[turn_index, member] = send_d[turn_index, member]

    def at_slots(turn_index):
        wait_bytes(recv_d.at[turn_index], GROUP - 1, recv_sem.at[turn_index, 3])
        arrived = recv_d[turn_index].astype(F32)
        around = jnp.concatenate(
            [arrived[:, 8 * pair : 8 * pair + 8, :].reshape(NT, 128) for pair in range(4)], axis=1
        ).astype(BF16)
        picked = dot(around, plane[...])
        return jnp.sum(picked * time_rows[...], axis=0, keepdims=True)

    spread_out(0, start, None)

    for load in loads[6:]:
        load.wait()
    edge_index = iota((NY, NY), 0)
    slot = edge_index & 63
    slot_x = third(slot)
    slot_y = slot - 3 * slot_x
    cell_y = (edge_index >> 6) * YS + jnp.where(slot_y == 0, -1, YS - 1 + slot_y)
    cell_y = jnp.where(slot < 21, cell_y, -1)
    select[...] = (cell_y == iota((NY, NY), 1)).astype(F32).astype(BF16)
    ky = ky_ref[...]
    mix_y[:NY, :] = ky
    mix_y[NY:, :] = dot(select[...], ky).astype(BF16)
    wide_row = iota((NY, NX), 0)
    wide_x = 2 * (wide_row & 3) + ((wide_row >> 2) & 1)
    cell_x = (wide_row >> 3) * XS - 1 + wide_x
    cell_x = jnp.where(wide_x < 7, cell_x, -1)
    widen = (cell_x == iota((NY, NX), 1)).astype(F32).astype(BF16)
    mix_x[...] = dot_rows(dot(widen, kx_ref[...]).astype(BF16), widen).astype(BF16)

    mix_along_y(0, arrived_blocks(0), None)
    send_field(0, dot(mix_x[...], grid_columns(0)))
    field_back(0)
    image_0 = at_slots(0) + noise * start

    sums = sum_row(
        lane_sum(start * start),
        lane_sum(start * image_0),
        lane_sum(image_0 * image_0),
        lane_sum(noise * start * image_0),
        lane_sum(noise * image_0 * image_0),
    )
    own = totals_of(sums, 2)
    spread_out(1, image_0 - quotient(own[1], own[0]) * start, group_tile(sums))
    spread_plain(image_0)
    blocks = arrived_blocks(1)
    member_sums = group_rows(recv_a[1])
    group_sums = jnp.sum(member_sums, axis=0, keepdims=True)
    members = totals_of(member_sums, 2)
    group = totals_of(group_sums, 2)
    part = quotient(members[1], members[0]) - quotient(group[1], group[0])
    blocks = [
        blocks[place] + part[place : place + 1, :] * recv_a[0, place].astype(F32)
        for place in range(GROUP)
    ]
    mix_along_y(1, blocks, chip_tile(group_sums))
    fold_plain()
    grid_columns(1)
    chip_sums = chip_rows(recv_b[1])
    chips = totals_of(chip_sums, 2)
    rr, along, square, noise_01, noise_11 = totals_of(
        jnp.sum(chip_sums, axis=0, keepdims=True), 5
    )
    step_0 = rr / along
    grow = step_0 * (square / along)
    ratio = jnp.maximum(grow - 1.0, 0.0)
    new = rr * ratio
    part = grow - step_0 * quotient(chips[1], chips[0])
    columns = jnp.concatenate(
        [
            part[place : place + 1, :] * recv_b[0, place].astype(F32)
            - step_0 * recv_b[1, place].astype(F32)
            for place in range(CHIPS)
        ],
        axis=0,
    )
    field = dot(mix_x[...], columns.astype(BF16))
    send_field(1, field)
    inner = jnp.sum(jnp.sum(field * spread_columns(), axis=0, keepdims=True), axis=1, keepdims=True)
    inner = jnp.broadcast_to(inner, (8, 128))
    sums_sent[0] = inner
    sums_group[member] = inner
    copy_group(lambda place: sums_sent.at[0], sums_group, sum_sem.at[2], sum_sem.at[3])
    field_back(1)
    wait_bytes(sums_group, GROUP - 1, sum_sem.at[3])
    inner = jnp.sum(sums_group[...], axis=0)
    sums_sent[1] = inner
    sums_chips[chip] = inner
    copy_chips(lambda place: sums_sent.at[1], sums_chips, sum_sem.at[0], sum_sem.at[1])
    direction = grow * start - step_0 * image_0
    image_1 = at_slots(1) + noise * direction
    wait_bytes(sums_chips, CHIPS - 1, sum_sem.at[1])
    inner = jnp.sum(sums_chips[...], axis=0)[:1, :1]
    curvature = -step_0 * (inner + grow * noise_01 - step_0 * noise_11)
    step_1 = new / curvature
    solved = step_0 * start + step_1 * direction
    rest = start - step_0 * image_0 - step_1 * image_1
    for k in range(TILES):
        result_ref[0, 0, 0, k : k + 1, :] = solved[:, CAP * k : CAP * (k + 1)]
        result_ref[1, 0, 0, k : k + 1, :] = rest[:, CAP * k : CAP * (k + 1)]

    for turn_index in range(ITERS):
        wait_bytes(recv_a.at[turn_index], GROUP - 1, send_sem.at[turn_index, 0])
        wait_bytes(recv_b.at[turn_index], CHIPS - 1, send_sem.at[turn_index, 1])
        wait_bytes(recv_c.at[turn_index], CHIPS - 1, send_sem.at[turn_index, 2])
        wait_bytes(recv_d.at[turn_index], GROUP - 1, send_sem.at[turn_index, 3])
    wait_bytes(recv_ga, GROUP - 1, plain_sem.at[0])
    wait_bytes(recv_gb, CHIPS - 1, plain_sem.at[2])
    wait_bytes(sums_chips, CHIPS - 1, sum_sem.at[0])
    wait_bytes(sums_group, GROUP - 1, sum_sem.at[2])


def per_device(cells, offsets, counts, observed, noise, kernel_x, kernel_y, kernel_t):
    vmem = pl.BlockSpec(memory_space=pltpu.VMEM)
    whole = pl.BlockSpec(memory_space=pltpu.HBM)
    group_block = pltpu.VMEM((ITERS, GROUP, 32, 128), BF16)
    chip_block = pltpu.VMEM((ITERS, CHIPS, 16, 128), BF16)
    time_block = pltpu.VMEM((ITERS, 8, 4, 16, 128), BF16)
    operands = (cells, offsets, counts, observed, noise, kernel_x, kernel_y, kernel_t)
    result = pl.pallas_call(
        kernel,
        out_shape=jax.ShapeDtypeStruct((2, *observed.shape), F32),
        in_specs=[whole] * 8,
        out_specs=vmem,
        scratch_shapes=[pltpu.VMEM(operand.shape, operand.dtype) for operand in operands]
        + [
            pltpu.VMEM((NY, SLOTS), BF16),
            pltpu.VMEM((NT, SLOTS), F32),
            pltpu.VMEM((NT, SLOTS), F32),
            pltpu.VMEM((2 * NY, NY), BF16),
            pltpu.VMEM((NY, NY), BF16),
            pltpu.VMEM((NY, NY), BF16),
            pltpu.VMEM((4, NT, 128), F32),
            group_block,
            group_block,
            time_block,
            chip_block,
            chip_block,
            chip_block,
            group_block,
            group_block,
            pltpu.VMEM((GROUP, 32, 128), BF16),
            pltpu.VMEM((GROUP, 32, 128), BF16),
            pltpu.VMEM((8, 4, 16, 128), BF16),
            pltpu.VMEM((CHIPS, 16, 128), BF16),
            pltpu.VMEM((2, 8, 128), F32),
            pltpu.VMEM((CHIPS, 8, 128), F32),
            pltpu.VMEM((GROUP, 8, 128), F32),
            pltpu.SemaphoreType.DMA((8,)),
            pltpu.SemaphoreType.DMA((ITERS, 4)),
            pltpu.SemaphoreType.DMA((ITERS, 4)),
            pltpu.SemaphoreType.DMA((4,)),
            pltpu.SemaphoreType.DMA((4,)),
            pltpu.SemaphoreType.REGULAR,
        ],
        compiler_params=pltpu.CompilerParams(
            collective_id=0, has_side_effects=True, vmem_limit_bytes=63 * 1024 * 1024
        ),
    )(*operands)
    return result[0], result[1]


def solution(mesh):
    placed = (
        P(None, "gx", "gy", None, None),
        P(None, "gx", "gy", None, None),
        P("gx", "gy", None),
        P("gx", "gy", None, None),
        P("gx", "gy", None, None),
        P(),
        P(),
        P(),
    )
    return jax.shard_map(
        per_device,
        mesh=mesh,
        in_specs=placed,
        out_specs=(P("gx", "gy", None, None), P("gx", "gy", None, None)),
        check_vma=False,
    )
```

```python
import jax
import jax.numpy as jnp
from jax import lax
from jax.experimental import pallas as pl
from jax.experimental.pallas import tpu as pltpu
from jax.sharding import PartitionSpec as P

XS = 4
YS = 64
ITERS = 2
TILES = 4
CAP = 256
SLOTS = TILES * CAP
CHIPS = 32
GROUP = 16
NX = 256
NY = 512
NT = 128
F32 = jnp.float32
BF16 = jnp.bfloat16
MESH = pl.DeviceIdType.MESH
ROW_ROW = (((1,), (1,)), ((), ()))
FAR_X = (2, 1, 3, 0)
FREE = 88


def cubic_weights(fraction):
    square = fraction * fraction
    cubic_term = square * fraction
    return (
        (2.0 * square - cubic_term - fraction) * 0.5,
        (3.0 * cubic_term - 5.0 * square + 2.0) * 0.5,
        (4.0 * square - 3.0 * cubic_term + fraction) * 0.5,
        (cubic_term - square) * 0.5,
    )


def iota(shape, axis):
    return lax.broadcasted_iota(jnp.int32, shape, axis)


def flat(rows):
    return jnp.concatenate([rows[k : k + 1, :] for k in range(TILES)], axis=1)


def dot(left, right):
    return jnp.dot(left, right, preferred_element_type=F32)


def dot_rows(left, right):
    return lax.dot_general(left, right, ROW_ROW, preferred_element_type=F32)


def spread_rows(weights, first, rows):
    total = jnp.zeros(rows.shape, F32)
    for shift in range(4):
        total = total + jnp.where(first + shift == rows, weights[shift], 0.0)
    return total


def third(index):
    return (index * 43) >> 7


def lane_sum(row):
    total = row[:, :128]
    for part in range(1, SLOTS // 128):
        total = total + row[:, 128 * part : 128 * (part + 1)]
    return total


def sum_row(*rows):
    lanes = iota((1, 128), 1)
    total = jnp.zeros((1, 128), F32)
    for k, row in enumerate(rows):
        total = jnp.where(lanes == FREE + k, jnp.sum(row, axis=1, keepdims=True), total)
    return total


def totals_of(row, count):
    return [
        jnp.sum(jnp.where(iota(row.shape, 1) == FREE + k, row, 0.0), axis=1, keepdims=True)
        for k in range(count)
    ]


def pieces(row):
    high = row.astype(BF16).astype(F32)
    middle = (row - high).astype(BF16).astype(F32)
    return high, middle, (row - high - middle).astype(BF16).astype(F32)


def group_tile(row):
    rows = iota((8, 128), 0)
    tile = jnp.zeros((8, 128), F32)
    for k, piece in enumerate(pieces(row)):
        tile = jnp.where(rows == k, piece, tile)
    return tile


def chip_tile(row):
    high, middle, low = pieces(row)
    rows = iota((16, 128), 0)
    tile = jnp.where(rows == 7, high + pltpu.roll(low, 8, 1), 0.0)
    return jnp.where(rows == 15, middle, tile)


def group_rows(received):
    rows = []
    for member in range(GROUP):
        tile = received[member, 16:, :].astype(F32)
        rows.append(tile[8:9, :] + tile[9:10, :] + tile[10:11, :])
    return jnp.concatenate(rows, axis=0)


def chip_rows(received):
    rows = []
    for chip in range(CHIPS):
        tile = received[chip].astype(F32)
        rows.append(tile[7:8, :] + tile[15:16, :] + pltpu.roll(tile[7:8, :], 120, 1))
    return jnp.concatenate(rows, axis=0)


def quotient(above, below):
    return jnp.where(below > 0.0, above / jnp.where(below > 0.0, below, 1.0), 0.0)


def kernel(
    cells_hbm,
    offsets_hbm,
    counts_hbm,
    observed_hbm,
    noise_hbm,
    kx_hbm,
    ky_hbm,
    kt_hbm,
    result_ref,
    cells_ref,
    offsets_ref,
    counts_ref,
    observed_ref,
    noise_ref,
    kx_ref,
    ky_ref,
    kt_ref,
    plane,
    time_rows,
    mixed_rows,
    mix_y,
    mix_x,
    select,
    turn,
    send_a,
    recv_a,
    send_b,
    recv_b,
    send_c,
    recv_c,
    send_d,
    recv_d,
    send_ga,
    recv_ga,
    send_gb,
    recv_gb,
    sums_sent,
    sums_chips,
    sums_group,
    load_sem,
    send_sem,
    recv_sem,
    plain_sem,
    sum_sem,
    entered,
):
    block_x = lax.axis_index("gx")
    block_y = lax.axis_index("gy")
    chip = block_x // 2
    core = block_x % 2
    chip_x = chip // 8
    chip_y = chip % 8
    member = block_y * 2 + core

    def far(step):
        return 4 + (step // 2) * (1 - step % 2) - ((step + 1) // 2) * (step % 2)

    def each_of_group(act):
        def one(step, carry):
            z = (block_y + far(step)) % 8
            act(z * 2 + 1 - core, (chip * 2 + 1 - core, z))
            return carry

        def same(step, carry):
            z = (block_y + far(step)) % 8
            act(z * 2 + core, (chip * 2 + core, z))
            return carry

        lax.fori_loop(0, 7, one, 0)
        lax.fori_loop(0, 7, same, 0)
        act(block_y * 2 + 1 - core, (chip * 2 + 1 - core, block_y))

    def each_of_chips(act):
        def one(step, carry):
            y = (chip_y + far(step)) % 8
            for shift in FAR_X:
                place = (chip_x + shift) % 4 * 8 + y
                act(place, (place * 2 + core, block_y))
            return carry

        lax.fori_loop(0, 7, one, 0)
        for shift in FAR_X[:3]:
            place = (chip_x + shift) % 4 * 8 + chip_y
            act(place, (place * 2 + core, block_y))

    barrier = pltpu.get_barrier_semaphore()

    def greet(place, device):
        pl.semaphore_signal(barrier, inc=1, device_id=device, device_id_type=MESH)

    def greet_row(act):
        for shift in FAR_X[:3]:
            place = (chip_x + shift) % 4 * 8 + chip_y
            act(place, (place * 2 + core, block_y))

    def greet_column(act):
        def one(step, carry):
            place = chip_x * 8 + (chip_y + far(step)) % 8
            act(place, (place * 2 + core, block_y))
            return carry

        lax.fori_loop(0, 7, one, 0)

    def greet_again(place, device):
        pl.semaphore_signal(entered, inc=1, device_id=device, device_id_type=MESH)

    for step in (4, 3, 5, 2, 6, 1, 7):
        for other in (0, 1):
            z = (block_y + step) % 8
            greet(None, (chip * 2 + other, z))
    greet(None, (chip * 2 + 1 - core, block_y))
    for step in (4, 3, 5, 2, 6, 1, 7):
        place = chip_x * 8 + (chip_y + step) % 8
        greet(None, (place * 2 + core, block_y))
    greet_row(greet)
    loads = [
        pltpu.make_async_copy(source, target, load_sem.at[k])
        for k, (source, target) in enumerate(
            (
                (cells_hbm, cells_ref),
                (offsets_hbm, offsets_ref),
                (counts_hbm, counts_ref),
                (observed_hbm, observed_ref),
                (noise_hbm, noise_ref),
                (kt_hbm, kt_ref),
                (ky_hbm, ky_ref),
                (kx_hbm, kx_ref),
            )
        )
    ]
    for load in loads:
        load.start()
    for load in loads[:6]:
        load.wait()

    live = jnp.concatenate(
        [
            (iota((1, CAP), 1) < counts_ref[0, :, k : k + 1]).astype(F32)
            for k in range(TILES)
        ],
        axis=1,
    )
    noise = flat(noise_ref[0, 0])
    start = live * flat(observed_ref[0, 0])
    weights_x = cubic_weights(flat(offsets_ref[0, 0, 0]))
    weights_y = cubic_weights(flat(offsets_ref[1, 0, 0]))
    weights_t = cubic_weights(flat(offsets_ref[2, 0, 0]))
    first_x = flat(cells_ref[0, 0, 0]) - XS * block_x
    first_y = flat(cells_ref[1, 0, 0]) - YS * block_y
    first_t = flat(cells_ref[2, 0, 0]) - 1
    rows_y = spread_rows(weights_y, first_y, iota((YS, SLOTS), 0) + 1)
    for x in range(7):
        row_x = spread_rows(weights_x, first_x, jnp.full((1, SLOTS), x, jnp.int32))
        plane[x * YS : (x + 1) * YS, :] = (row_x * rows_y).astype(BF16)
    edge_row = iota((YS, SLOTS), 0)
    edge_x = third(edge_row)
    edge_y = edge_row - 3 * edge_x
    edge_y = jnp.where(edge_y == 0, 0, YS + edge_y)
    plane[7 * YS :, :] = (
        spread_rows(weights_x, first_x, edge_x) * spread_rows(weights_y, first_y, edge_y)
    ).astype(BF16)
    rows_t = spread_rows(weights_t, first_t, iota((NT, SLOTS), 0)) * live
    time_rows[...] = rows_t
    high = rows_t.astype(BF16)
    low = (rows_t - high.astype(F32)).astype(BF16)
    kt = kt_ref[...]
    mixed_rows[...] = dot(kt, high) + dot(kt, low)

    low_half = iota((32, 128), 1) < 64
    edge_lane = third(iota((8, NY), 1) & 63)

    def wait_bytes(ref, count, semaphore):
        block = ref.at[pl.ds(0, count)]
        pltpu.make_async_copy(block, block, semaphore).wait()

    def copy_group(source, target, sent, received):
        def act(place, device):
            pltpu.make_async_remote_copy(
                src_ref=source(place),
                dst_ref=target.at[member],
                send_sem=sent,
                recv_sem=received,
                device_id=device,
                device_id_type=MESH,
            ).start()

        each_of_group(act)

    def copy_chips(source, target, sent, received):
        def act(place, device):
            pltpu.make_async_remote_copy(
                src_ref=source(place),
                dst_ref=target.at[chip],
                send_sem=sent,
                recv_sem=received,
                device_id=device,
                device_id_type=MESH,
            ).start()

        each_of_chips(act)

    def time_blocks(spread, tile):
        blocks = [
            spread[:, 128 * pair : 128 * (pair + 1)].reshape(GROUP, 8, 128) for pair in range(4)
        ]
        if tile is not None:
            blocks[3] = blocks[3] + tile[None]
        return jnp.concatenate(blocks, axis=1).astype(BF16)

    def whole_rows(received):
        columns = []
        for pair in range(4):
            parts = []
            for half in range(2):
                lower = received[4 * pair + half]
                upper = received[4 * pair + 2 + half]
                parts.append(jnp.where(low_half, lower, pltpu.roll(upper, 64, 1)))
                parts.append(jnp.where(low_half, pltpu.roll(lower, 64, 1), upper))
            columns.append(jnp.concatenate(parts, axis=0))
        main = jnp.concatenate(columns, axis=1)
        zero = jnp.zeros((8, NY), F32)
        main_parts, edge_parts = [], []
        for half in range(2):
            edge = main[64 * half + 56 : 64 * half + 64, :]
            main_parts.append(main[64 * half : 64 * half + 56, :])
            main_parts.append(zero)
            for row in range(7):
                x = 2 * (row % 4) + row // 4
                edge_parts.append(jnp.where(edge_lane == x, edge, 0.0))
            edge_parts.append(zero)
        return jnp.concatenate(main_parts, axis=0), jnp.concatenate(edge_parts, axis=0)

    def to_column_blocks(rows, target, tile):
        for row in range(16):
            for quarter in range(4):
                turn[quarter, pl.ds(row, 8, stride=16), :] = rows[
                    8 * row : 8 * row + 8, 128 * quarter : 128 * (quarter + 1)
                ]
        for quarter in range(4):
            blocks = turn[quarter, :NT, :].reshape(8, 16, 128)
            if tile is not None:
                blocks = blocks + tile[None]
            target[:, quarter] = blocks.astype(BF16)

    def spread_out(turn_index, vector, tile):
        weighted = (mixed_rows[...] * vector).astype(BF16)
        send_a[turn_index] = time_blocks(dot_rows(weighted, plane[...]), tile)
        if turn_index == 0:
            pl.semaphore_wait(barrier, GROUP - 1 + 7 + 3)
        copy_group(
            lambda place: send_a.at[turn_index, place],
            recv_a.at[turn_index],
            send_sem.at[turn_index, 0],
            recv_sem.at[turn_index, 0],
        )
        if turn_index == 0:
            greet_row(greet_again)
        recv_a[turn_index, member] = send_a[turn_index, member]

    def spread_plain(vector):
        weighted = (time_rows[...] * vector).astype(BF16)
        send_ga[...] = time_blocks(dot_rows(weighted, plane[...]), None)
        copy_group(lambda place: send_ga.at[place], recv_ga, plain_sem.at[0], plain_sem.at[1])
        recv_ga[member] = send_ga[member]

    def arrived_blocks(turn_index):
        wait_bytes(recv_a.at[turn_index], GROUP - 1, recv_sem.at[turn_index, 0])
        return [recv_a[turn_index, place].astype(F32) for place in range(GROUP)]

    def mix_along_y(turn_index, blocks, tile):
        main, edge = whole_rows(blocks)
        left = jnp.concatenate([main, edge], axis=1).astype(BF16)
        to_column_blocks(dot(left, mix_y[...]), send_b.at[turn_index], tile)
        if turn_index == 0:
            pl.semaphore_wait(entered, 3)
        copy_chips(
            lambda place: send_b.at[turn_index, place // 4, place % 4],
            recv_b.at[turn_index],
            send_sem.at[turn_index, 1],
            recv_sem.at[turn_index, 1],
        )
        recv_b[turn_index, chip] = send_b[turn_index, chip // 4, chip % 4]

    def fold_plain():
        wait_bytes(recv_ga, GROUP - 1, plain_sem.at[1])
        main, edge = whole_rows([recv_ga[place].astype(F32) for place in range(GROUP)])
        to_column_blocks(main + dot(edge.astype(BF16), select[...]), send_gb, None)
        copy_chips(
            lambda place: send_gb.at[place // 4, place % 4],
            recv_gb,
            plain_sem.at[2],
            plain_sem.at[3],
        )
        recv_gb[chip] = send_gb[chip // 4, chip % 4]

    def grid_columns(turn_index):
        wait_bytes(recv_b.at[turn_index], CHIPS - 1, recv_sem.at[turn_index, 1])
        return recv_b[turn_index].reshape(NY, 128)

    def spread_columns():
        wait_bytes(recv_gb, CHIPS - 1, plain_sem.at[3])
        return recv_gb[...].reshape(NY, 128).astype(F32)

    def send_field(turn_index, field):
        send_c[turn_index] = field.astype(BF16).reshape(CHIPS, 16, 128)
        copy_chips(
            lambda place: send_c.at[turn_index, place],
            recv_c.at[turn_index],
            send_sem.at[turn_index, 2],
            recv_sem.at[turn_index, 2],
        )
        recv_c[turn_index, chip] = send_c[turn_index, chip]

    def field_back(turn_index):
        wait_bytes(recv_c.at[turn_index], CHIPS - 1, recv_sem.at[turn_index, 2])
        for time in range(8):
            for quarter in range(4):
                turn[quarter, 16 * time : 16 * time + 16, :] = recv_c[
                    turn_index, 4 * time + quarter
                ].astype(F32)
        rows = [
            jnp.concatenate(
                [turn[quarter, pl.ds(row, 8, stride=16), :] for quarter in range(4)], axis=1
            )
            for row in range(16)
        ]
        edges = dot_rows(jnp.concatenate(rows, axis=0).astype(BF16), select[...])
        for half in range(2):
            edge = jnp.zeros((8, NY), F32)
            for row in range(7):
                x = 2 * (row % 4) + row // 4
                first = 64 * half + 8 * row
                edge = edge + jnp.where(edge_lane == x, edges[first : first + 8, :], 0.0)
            even = jnp.concatenate(rows[8 * half : 8 * half + 4], axis=0)
            odd = jnp.concatenate(rows[8 * half + 4 : 8 * half + 7] + [edge], axis=0)
            for pair in range(4):
                lanes = slice(128 * pair, 128 * (pair + 1))
                lower = jnp.where(low_half, even[:, lanes], pltpu.roll(odd[:, lanes], 64, 1))
                upper = jnp.where(low_half, pltpu.roll(even[:, lanes], 64, 1), odd[:, lanes])
                send_d[turn_index, 4 * pair + half] = lower.astype(BF16)
                send_d[turn_index, 4 * pair + 2 + half] = upper.astype(BF16)
        copy_group(
            lambda place: send_d.at[turn_index, place],
            recv_d.at[turn_index],
            send_sem.at[turn_index, 3],
            recv_sem.at[turn_index, 3],
        )
        recv_d[turn_index, member] = send_d[turn_index, member]

    def at_slots(turn_index):
        wait_bytes(recv_d.at[turn_index], GROUP - 1, recv_sem.at[turn_index, 3])
        arrived = recv_d[turn_index].astype(F32)
        around = jnp.concatenate(
            [arrived[:, 8 * pair : 8 * pair + 8, :].reshape(NT, 128) for pair in range(4)], axis=1
        ).astype(BF16)
        picked = dot(around, plane[...])
        return jnp.sum(picked * time_rows[...], axis=0, keepdims=True)

    spread_out(0, start, None)

    for load in loads[6:]:
        load.wait()
    edge_index = iota((NY, NY), 0)
    slot = edge_index & 63
    slot_x = third(slot)
    slot_y = slot - 3 * slot_x
    cell_y = (edge_index >> 6) * YS + jnp.where(slot_y == 0, -1, YS - 1 + slot_y)
    cell_y = jnp.where(slot < 21, cell_y, -1)
    select[...] = (cell_y == iota((NY, NY), 1)).astype(F32).astype(BF16)
    ky = ky_ref[...]
    mix_y[:NY, :] = ky
    mix_y[NY:, :] = dot(select[...], ky).astype(BF16)
    wide_row = iota((NY, NX), 0)
    wide_x = 2 * (wide_row & 3) + ((wide_row >> 2) & 1)
    cell_x = (wide_row >> 3) * XS - 1 + wide_x
    cell_x = jnp.where(wide_x < 7, cell_x, -1)
    widen = (cell_x == iota((NY, NX), 1)).astype(F32).astype(BF16)
    mix_x[...] = dot_rows(dot(widen, kx_ref[...]).astype(BF16), widen).astype(BF16)

    mix_along_y(0, arrived_blocks(0), None)
    send_field(0, dot(mix_x[...], grid_columns(0)))
    field_back(0)
    image_0 = at_slots(0) + noise * start

    sums = sum_row(
        lane_sum(start * start),
        lane_sum(start * image_0),
        lane_sum(image_0 * image_0),
        lane_sum(noise * start * image_0),
        lane_sum(noise * image_0 * image_0),
    )
    own = totals_of(sums, 2)
    spread_out(1, image_0 - quotient(own[1], own[0]) * start, group_tile(sums))
    spread_plain(image_0)
    blocks = arrived_blocks(1)
    member_sums = group_rows(recv_a[1])
    group_sums = jnp.sum(member_sums, axis=0, keepdims=True)
    members = totals_of(member_sums, 2)
    group = totals_of(group_sums, 2)
    part = quotient(members[1], members[0]) - quotient(group[1], group[0])
    blocks = [
        blocks[place] + part[place : place + 1, :] * recv_a[0, place].astype(F32)
        for place in range(GROUP)
    ]
    mix_along_y(1, blocks, chip_tile(group_sums))
    fold_plain()
    grid_columns(1)
    chip_sums = chip_rows(recv_b[1])
    chips = totals_of(chip_sums, 2)
    rr, along, square, noise_01, noise_11 = totals_of(
        jnp.sum(chip_sums, axis=0, keepdims=True), 5
    )
    step_0 = rr / along
    grow = step_0 * (square / along)
    ratio = jnp.maximum(grow - 1.0, 0.0)
    new = rr * ratio
    part = grow - step_0 * quotient(chips[1], chips[0])
    columns = jnp.concatenate(
        [
            part[place : place + 1, :] * recv_b[0, place].astype(F32)
            - step_0 * recv_b[1, place].astype(F32)
            for place in range(CHIPS)
        ],
        axis=0,
    )
    field = dot(mix_x[...], columns.astype(BF16))
    send_field(1, field)
    inner = jnp.sum(jnp.sum(field * spread_columns(), axis=0, keepdims=True), axis=1, keepdims=True)
    inner = jnp.broadcast_to(inner, (8, 128))
    sums_sent[0] = inner
    sums_group[member] = inner
    copy_group(lambda place: sums_sent.at[0], sums_group, sum_sem.at[2], sum_sem.at[3])
    field_back(1)
    wait_bytes(sums_group, GROUP - 1, sum_sem.at[3])
    inner = jnp.sum(sums_group[...], axis=0)
    sums_sent[1] = inner
    sums_chips[chip] = inner
    copy_chips(lambda place: sums_sent.at[1], sums_chips, sum_sem.at[0], sum_sem.at[1])
    direction = grow * start - step_0 * image_0
    image_1 = at_slots(1) + noise * direction
    wait_bytes(sums_chips, CHIPS - 1, sum_sem.at[1])
    inner = jnp.sum(sums_chips[...], axis=0)[:1, :1]
    curvature = -step_0 * (inner + grow * noise_01 - step_0 * noise_11)
    step_1 = new / curvature
    solved = step_0 * start + step_1 * direction
    rest = start - step_0 * image_0 - step_1 * image_1
    for k in range(TILES):
        result_ref[0, 0, 0, k : k + 1, :] = solved[:, CAP * k : CAP * (k + 1)]
        result_ref[1, 0, 0, k : k + 1, :] = rest[:, CAP * k : CAP * (k + 1)]

    for turn_index in range(ITERS):
        wait_bytes(recv_a.at[turn_index], GROUP - 1, send_sem.at[turn_index, 0])
        wait_bytes(recv_b.at[turn_index], CHIPS - 1, send_sem.at[turn_index, 1])
        wait_bytes(recv_c.at[turn_index], CHIPS - 1, send_sem.at[turn_index, 2])
        wait_bytes(recv_d.at[turn_index], GROUP - 1, send_sem.at[turn_index, 3])
    wait_bytes(recv_ga, GROUP - 1, plain_sem.at[0])
    wait_bytes(recv_gb, CHIPS - 1, plain_sem.at[2])
    wait_bytes(sums_chips, CHIPS - 1, sum_sem.at[0])
    wait_bytes(sums_group, GROUP - 1, sum_sem.at[2])


def per_device(cells, offsets, counts, observed, noise, kernel_x, kernel_y, kernel_t):
    vmem = pl.BlockSpec(memory_space=pltpu.VMEM)
    whole = pl.BlockSpec(memory_space=pltpu.HBM)
    group_block = pltpu.VMEM((ITERS, GROUP, 32, 128), BF16)
    chip_block = pltpu.VMEM((ITERS, CHIPS, 16, 128), BF16)
    time_block = pltpu.VMEM((ITERS, 8, 4, 16, 128), BF16)
    operands = (cells, offsets, counts, observed, noise, kernel_x, kernel_y, kernel_t)
    result = pl.pallas_call(
        kernel,
        out_shape=jax.ShapeDtypeStruct((2, *observed.shape), F32),
        in_specs=[whole] * 8,
        out_specs=vmem,
        scratch_shapes=[pltpu.VMEM(operand.shape, operand.dtype) for operand in operands]
        + [
            pltpu.VMEM((NY, SLOTS), BF16),
            pltpu.VMEM((NT, SLOTS), F32),
            pltpu.VMEM((NT, SLOTS), F32),
            pltpu.VMEM((2 * NY, NY), BF16),
            pltpu.VMEM((NY, NY), BF16),
            pltpu.VMEM((NY, NY), BF16),
            pltpu.VMEM((4, NT + 16, 128), F32),
            group_block,
            group_block,
            time_block,
            chip_block,
            chip_block,
            chip_block,
            group_block,
            group_block,
            pltpu.VMEM((GROUP, 32, 128), BF16),
            pltpu.VMEM((GROUP, 32, 128), BF16),
            pltpu.VMEM((8, 4, 16, 128), BF16),
            pltpu.VMEM((CHIPS, 16, 128), BF16),
            pltpu.VMEM((2, 8, 128), F32),
            pltpu.VMEM((CHIPS, 8, 128), F32),
            pltpu.VMEM((GROUP, 8, 128), F32),
            pltpu.SemaphoreType.DMA((8,)),
            pltpu.SemaphoreType.DMA((ITERS, 4)),
            pltpu.SemaphoreType.DMA((ITERS, 4)),
            pltpu.SemaphoreType.DMA((4,)),
            pltpu.SemaphoreType.DMA((4,)),
            pltpu.SemaphoreType.REGULAR,
        ],
        compiler_params=pltpu.CompilerParams(
            collective_id=0, has_side_effects=True, vmem_limit_bytes=63 * 1024 * 1024
        ),
    )(*operands)
    return result[0], result[1]


def solution(mesh):
    placed = (
        P(None, "gx", "gy", None, None),
        P(None, "gx", "gy", None, None),
        P("gx", "gy", None),
        P("gx", "gy", None, None),
        P("gx", "gy", None, None),
        P(),
        P(),
        P(),
    )
    return jax.shard_map(
        per_device,
        mesh=mesh,
        in_specs=placed,
        out_specs=(P("gx", "gy", None, None), P("gx", "gy", None, None)),
        check_vma=False,
    )
```

```python
import jax
import jax.numpy as jnp
from jax import lax
from jax.experimental import pallas as pl
from jax.experimental.pallas import tpu as pltpu
from jax.sharding import PartitionSpec as P

XS = 4
YS = 64
ITERS = 2
TILES = 4
CAP = 256
SLOTS = TILES * CAP
CHIPS = 32
GROUP = 16
NX = 256
NY = 512
NT = 128
F32 = jnp.float32
BF16 = jnp.bfloat16
MESH = pl.DeviceIdType.MESH
ROW_ROW = (((1,), (1,)), ((), ()))
FAR_X = (2, 1, 3, 0)
FREE = 88


def cubic_weights(fraction):
    square = fraction * fraction
    cubic_term = square * fraction
    return (
        (2.0 * square - cubic_term - fraction) * 0.5,
        (3.0 * cubic_term - 5.0 * square + 2.0) * 0.5,
        (4.0 * square - 3.0 * cubic_term + fraction) * 0.5,
        (cubic_term - square) * 0.5,
    )


def iota(shape, axis):
    return lax.broadcasted_iota(jnp.int32, shape, axis)


def flat(rows):
    return jnp.concatenate([rows[k : k + 1, :] for k in range(TILES)], axis=1)


def dot(left, right):
    return jnp.dot(left, right, preferred_element_type=F32)


def dot_rows(left, right):
    return lax.dot_general(left, right, ROW_ROW, preferred_element_type=F32)


def spread_rows(weights, first, rows):
    total = jnp.zeros(rows.shape, F32)
    for shift in range(4):
        total = total + jnp.where(first + shift == rows, weights[shift], 0.0)
    return total


def third(index):
    return (index * 43) >> 7


def lane_sum(row):
    total = row[:, :128]
    for part in range(1, SLOTS // 128):
        total = total + row[:, 128 * part : 128 * (part + 1)]
    return total


def sum_row(*rows):
    lanes = iota((1, 128), 1)
    total = jnp.zeros((1, 128), F32)
    for k, row in enumerate(rows):
        total = jnp.where(lanes == FREE + k, jnp.sum(row, axis=1, keepdims=True), total)
    return total


def totals_of(row, count):
    return [
        jnp.sum(jnp.where(iota(row.shape, 1) == FREE + k, row, 0.0), axis=1, keepdims=True)
        for k in range(count)
    ]


def pieces(row):
    high = row.astype(BF16).astype(F32)
    middle = (row - high).astype(BF16).astype(F32)
    return high, middle, (row - high - middle).astype(BF16).astype(F32)


def group_tile(row):
    rows = iota((8, 128), 0)
    tile = jnp.zeros((8, 128), F32)
    for k, piece in enumerate(pieces(row)):
        tile = jnp.where(rows == k, piece, tile)
    return tile


def chip_tile(row):
    high, middle, low = pieces(row)
    rows = iota((16, 128), 0)
    tile = jnp.where(rows == 7, high + pltpu.roll(low, 8, 1), 0.0)
    return jnp.where(rows == 15, middle, tile)


def group_rows(received):
    rows = []
    for member in range(GROUP):
        tile = received[member, 16:, :].astype(F32)
        rows.append(tile[8:9, :] + tile[9:10, :] + tile[10:11, :])
    return jnp.concatenate(rows, axis=0)


def chip_rows(received):
    rows = []
    for chip in range(CHIPS):
        tile = received[chip].astype(F32)
        rows.append(tile[7:8, :] + tile[15:16, :] + pltpu.roll(tile[7:8, :], 120, 1))
    return jnp.concatenate(rows, axis=0)


def quotient(above, below):
    return jnp.where(below > 0.0, above / jnp.where(below > 0.0, below, 1.0), 0.0)


def kernel(
    cells_hbm,
    offsets_hbm,
    counts_hbm,
    observed_hbm,
    noise_hbm,
    kx_hbm,
    ky_hbm,
    kt_hbm,
    result_ref,
    cells_ref,
    offsets_ref,
    counts_ref,
    observed_ref,
    noise_ref,
    kx_ref,
    ky_ref,
    kt_ref,
    plane,
    time_rows,
    mixed_rows,
    mix_y,
    mix_x,
    select,
    turn,
    send_a,
    recv_a,
    send_b,
    recv_b,
    send_c,
    recv_c,
    send_d,
    recv_d,
    send_ga,
    recv_ga,
    send_gb,
    recv_gb,
    sums_sent,
    sums_chips,
    sums_group,
    load_sem,
    send_sem,
    recv_sem,
    plain_sem,
    sum_sem,
    entered,
):
    block_x = lax.axis_index("gx")
    block_y = lax.axis_index("gy")
    chip = block_x // 2
    core = block_x % 2
    chip_x = chip // 8
    chip_y = chip % 8
    member = block_y * 2 + core

    def far(step):
        return 4 + (step // 2) * (1 - step % 2) - ((step + 1) // 2) * (step % 2)

    def each_of_group(act):
        def one(step, carry):
            z = (block_y + far(step)) % 8
            act(z * 2 + 1 - core, (chip * 2 + 1 - core, z))
            return carry

        def same(step, carry):
            z = (block_y + far(step)) % 8
            act(z * 2 + core, (chip * 2 + core, z))
            return carry

        lax.fori_loop(0, 7, one, 0)
        lax.fori_loop(0, 7, same, 0)
        act(block_y * 2 + 1 - core, (chip * 2 + 1 - core, block_y))

    def each_of_chips(act):
        def one(step, carry):
            y = (chip_y + far(step)) % 8
            for shift in FAR_X:
                place = (chip_x + shift) % 4 * 8 + y
                act(place, (place * 2 + core, block_y))
            return carry

        lax.fori_loop(0, 7, one, 0)
        for shift in FAR_X[:3]:
            place = (chip_x + shift) % 4 * 8 + chip_y
            act(place, (place * 2 + core, block_y))

    barrier = pltpu.get_barrier_semaphore()

    def greet(place, device):
        pl.semaphore_signal(barrier, inc=1, device_id=device, device_id_type=MESH)

    def greet_row(act):
        for shift in FAR_X[:3]:
            place = (chip_x + shift) % 4 * 8 + chip_y
            act(place, (place * 2 + core, block_y))

    def greet_column(act):
        def one(step, carry):
            place = chip_x * 8 + (chip_y + far(step)) % 8
            act(place, (place * 2 + core, block_y))
            return carry

        lax.fori_loop(0, 7, one, 0)

    def greet_again(place, device):
        pl.semaphore_signal(entered, inc=1, device_id=device, device_id_type=MESH)

    for step in (4, 3, 5, 2, 6, 1, 7):
        for other in (0, 1):
            z = (block_y + step) % 8
            greet(None, (chip * 2 + other, z))
    greet(None, (chip * 2 + 1 - core, block_y))
    loads = [
        pltpu.make_async_copy(source, target, load_sem.at[k])
        for k, (source, target) in enumerate(
            (
                (cells_hbm, cells_ref),
                (offsets_hbm, offsets_ref),
                (counts_hbm, counts_ref),
                (observed_hbm, observed_ref),
                (noise_hbm, noise_ref),
                (kt_hbm, kt_ref),
                (ky_hbm, ky_ref),
                (kx_hbm, kx_ref),
            )
        )
    ]
    for load in loads:
        load.start()
    for step in (4, 3, 5, 2, 6, 1, 7):
        place = chip_x * 8 + (chip_y + step) % 8
        greet(None, (place * 2 + core, block_y))
    greet_row(greet)
    for load in loads[:6]:
        load.wait()

    live = jnp.concatenate(
        [
            (iota((1, CAP), 1) < counts_ref[0, :, k : k + 1]).astype(F32)
            for k in range(TILES)
        ],
        axis=1,
    )
    noise = flat(noise_ref[0, 0])
    start = live * flat(observed_ref[0, 0])
    weights_x = cubic_weights(flat(offsets_ref[0, 0, 0]))
    weights_y = cubic_weights(flat(offsets_ref[1, 0, 0]))
    weights_t = cubic_weights(flat(offsets_ref[2, 0, 0]))
    first_x = flat(cells_ref[0, 0, 0]) - XS * block_x
    first_y = flat(cells_ref[1, 0, 0]) - YS * block_y
    first_t = flat(cells_ref[2, 0, 0]) - 1
    rows_y = spread_rows(weights_y, first_y, iota((YS, SLOTS), 0) + 1)
    for x in range(7):
        row_x = spread_rows(weights_x, first_x, jnp.full((1, SLOTS), x, jnp.int32))
        plane[x * YS : (x + 1) * YS, :] = (row_x * rows_y).astype(BF16)
    edge_row = iota((YS, SLOTS), 0)
    edge_x = third(edge_row)
    edge_y = edge_row - 3 * edge_x
    edge_y = jnp.where(edge_y == 0, 0, YS + edge_y)
    plane[7 * YS :, :] = (
        spread_rows(weights_x, first_x, edge_x) * spread_rows(weights_y, first_y, edge_y)
    ).astype(BF16)
    rows_t = spread_rows(weights_t, first_t, iota((NT, SLOTS), 0)) * live
    time_rows[...] = rows_t
    high = rows_t.astype(BF16)
    low = (rows_t - high.astype(F32)).astype(BF16)
    kt = kt_ref[...]
    mixed_rows[...] = dot(kt, high) + dot(kt, low)

    low_half = iota((32, 128), 1) < 64
    edge_lane = third(iota((8, NY), 1) & 63)

    def wait_bytes(ref, count, semaphore):
        block = ref.at[pl.ds(0, count)]
        pltpu.make_async_copy(block, block, semaphore).wait()

    def copy_group(source, target, sent, received):
        def act(place, device):
            pltpu.make_async_remote_copy(
                src_ref=source(place),
                dst_ref=target.at[member],
                send_sem=sent,
                recv_sem=received,
                device_id=device,
                device_id_type=MESH,
            ).start()

        each_of_group(act)

    def copy_chips(source, target, sent, received):
        def act(place, device):
            pltpu.make_async_remote_copy(
                src_ref=source(place),
                dst_ref=target.at[chip],
                send_sem=sent,
                recv_sem=received,
                device_id=device,
                device_id_type=MESH,
            ).start()

        each_of_chips(act)

    def time_blocks(spread, tile):
        blocks = [
            spread[:, 128 * pair : 128 * (pair + 1)].reshape(GROUP, 8, 128) for pair in range(4)
        ]
        if tile is not None:
            blocks[3] = blocks[3] + tile[None]
        return jnp.concatenate(blocks, axis=1).astype(BF16)

    def whole_rows(received):
        columns = []
        for pair in range(4):
            parts = []
            for half in range(2):
                lower = received[4 * pair + half]
                upper = received[4 * pair + 2 + half]
                parts.append(jnp.where(low_half, lower, pltpu.roll(upper, 64, 1)))
                parts.append(jnp.where(low_half, pltpu.roll(lower, 64, 1), upper))
            columns.append(jnp.concatenate(parts, axis=0))
        main = jnp.concatenate(columns, axis=1)
        zero = jnp.zeros((8, NY), F32)
        main_parts, edge_parts = [], []
        for half in range(2):
            edge = main[64 * half + 56 : 64 * half + 64, :]
            main_parts.append(main[64 * half : 64 * half + 56, :])
            main_parts.append(zero)
            for row in range(7):
                x = 2 * (row % 4) + row // 4
                edge_parts.append(jnp.where(edge_lane == x, edge, 0.0))
            edge_parts.append(zero)
        return jnp.concatenate(main_parts, axis=0), jnp.concatenate(edge_parts, axis=0)

    def to_column_blocks(rows, target, tile):
        for row in range(16):
            for quarter in range(4):
                turn[quarter, pl.ds(row, 8, stride=16), :] = rows[
                    8 * row : 8 * row + 8, 128 * quarter : 128 * (quarter + 1)
                ]
        for quarter in range(4):
            blocks = turn[quarter, :NT, :].reshape(8, 16, 128)
            if tile is not None:
                blocks = blocks + tile[None]
            target[:, quarter] = blocks.astype(BF16)

    def spread_out(turn_index, vector, tile):
        weighted = (mixed_rows[...] * vector).astype(BF16)
        send_a[turn_index] = time_blocks(dot_rows(weighted, plane[...]), tile)
        if turn_index == 0:
            pl.semaphore_wait(barrier, GROUP - 1 + 7 + 3)
        copy_group(
            lambda place: send_a.at[turn_index, place],
            recv_a.at[turn_index],
            send_sem.at[turn_index, 0],
            recv_sem.at[turn_index, 0],
        )
        if turn_index == 0:
            greet_row(greet_again)
        recv_a[turn_index, member] = send_a[turn_index, member]

    def spread_plain(vector):
        weighted = (time_rows[...] * vector).astype(BF16)
        send_ga[...] = time_blocks(dot_rows(weighted, plane[...]), None)
        copy_group(lambda place: send_ga.at[place], recv_ga, plain_sem.at[0], plain_sem.at[1])
        recv_ga[member] = send_ga[member]

    def arrived_blocks(turn_index):
        wait_bytes(recv_a.at[turn_index], GROUP - 1, recv_sem.at[turn_index, 0])
        return [recv_a[turn_index, place].astype(F32) for place in range(GROUP)]

    def mix_along_y(turn_index, blocks, tile):
        main, edge = whole_rows(blocks)
        left = jnp.concatenate([main, edge], axis=1).astype(BF16)
        to_column_blocks(dot(left, mix_y[...]), send_b.at[turn_index], tile)
        if turn_index == 0:
            pl.semaphore_wait(entered, 3)
        copy_chips(
            lambda place: send_b.at[turn_index, place // 4, place % 4],
            recv_b.at[turn_index],
            send_sem.at[turn_index, 1],
            recv_sem.at[turn_index, 1],
        )
        recv_b[turn_index, chip] = send_b[turn_index, chip // 4, chip % 4]

    def fold_plain():
        wait_bytes(recv_ga, GROUP - 1, plain_sem.at[1])
        main, edge = whole_rows([recv_ga[place].astype(F32) for place in range(GROUP)])
        to_column_blocks(main + dot(edge.astype(BF16), select[...]), send_gb, None)
        copy_chips(
            lambda place: send_gb.at[place // 4, place % 4],
            recv_gb,
            plain_sem.at[2],
            plain_sem.at[3],
        )
        recv_gb[chip] = send_gb[chip // 4, chip % 4]

    def grid_columns(turn_index):
        wait_bytes(recv_b.at[turn_index], CHIPS - 1, recv_sem.at[turn_index, 1])
        return recv_b[turn_index].reshape(NY, 128)

    def spread_columns():
        wait_bytes(recv_gb, CHIPS - 1, plain_sem.at[3])
        return recv_gb[...].reshape(NY, 128).astype(F32)

    def send_field(turn_index, field):
        send_c[turn_index] = field.astype(BF16).reshape(CHIPS, 16, 128)
        copy_chips(
            lambda place: send_c.at[turn_index, place],
            recv_c.at[turn_index],
            send_sem.at[turn_index, 2],
            recv_sem.at[turn_index, 2],
        )
        recv_c[turn_index, chip] = send_c[turn_index, chip]

    def field_back(turn_index):
        wait_bytes(recv_c.at[turn_index], CHIPS - 1, recv_sem.at[turn_index, 2])
        for time in range(8):
            for quarter in range(4):
                turn[quarter, 16 * time : 16 * time + 16, :] = recv_c[
                    turn_index, 4 * time + quarter
                ].astype(F32)
        rows = [
            jnp.concatenate(
                [turn[quarter, pl.ds(row, 8, stride=16), :] for quarter in range(4)], axis=1
            )
            for row in range(16)
        ]
        edges = dot_rows(jnp.concatenate(rows, axis=0).astype(BF16), select[...])
        for half in range(2):
            edge = jnp.zeros((8, NY), F32)
            for row in range(7):
                x = 2 * (row % 4) + row // 4
                first = 64 * half + 8 * row
                edge = edge + jnp.where(edge_lane == x, edges[first : first + 8, :], 0.0)
            even = jnp.concatenate(rows[8 * half : 8 * half + 4], axis=0)
            odd = jnp.concatenate(rows[8 * half + 4 : 8 * half + 7] + [edge], axis=0)
            for pair in range(4):
                lanes = slice(128 * pair, 128 * (pair + 1))
                lower = jnp.where(low_half, even[:, lanes], pltpu.roll(odd[:, lanes], 64, 1))
                upper = jnp.where(low_half, pltpu.roll(even[:, lanes], 64, 1), odd[:, lanes])
                send_d[turn_index, 4 * pair + half] = lower.astype(BF16)
                send_d[turn_index, 4 * pair + 2 + half] = upper.astype(BF16)
        copy_group(
            lambda place: send_d.at[turn_index, place],
            recv_d.at[turn_index],
            send_sem.at[turn_index, 3],
            recv_sem.at[turn_index, 3],
        )
        recv_d[turn_index, member] = send_d[turn_index, member]

    def at_slots(turn_index):
        wait_bytes(recv_d.at[turn_index], GROUP - 1, recv_sem.at[turn_index, 3])
        arrived = recv_d[turn_index].astype(F32)
        around = jnp.concatenate(
            [arrived[:, 8 * pair : 8 * pair + 8, :].reshape(NT, 128) for pair in range(4)], axis=1
        ).astype(BF16)
        picked = dot(around, plane[...])
        return jnp.sum(picked * time_rows[...], axis=0, keepdims=True)

    spread_out(0, start, None)

    for load in loads[6:]:
        load.wait()
    edge_index = iota((NY, NY), 0)
    slot = edge_index & 63
    slot_x = third(slot)
    slot_y = slot - 3 * slot_x
    cell_y = (edge_index >> 6) * YS + jnp.where(slot_y == 0, -1, YS - 1 + slot_y)
    cell_y = jnp.where(slot < 21, cell_y, -1)
    select[...] = (cell_y == iota((NY, NY), 1)).astype(F32).astype(BF16)
    ky = ky_ref[...]
    mix_y[:NY, :] = ky
    mix_y[NY:, :] = dot(select[...], ky).astype(BF16)
    wide_row = iota((NY, NX), 0)
    wide_x = 2 * (wide_row & 3) + ((wide_row >> 2) & 1)
    cell_x = (wide_row >> 3) * XS - 1 + wide_x
    cell_x = jnp.where(wide_x < 7, cell_x, -1)
    widen = (cell_x == iota((NY, NX), 1)).astype(F32).astype(BF16)
    mix_x[...] = dot_rows(dot(widen, kx_ref[...]).astype(BF16), widen).astype(BF16)

    mix_along_y(0, arrived_blocks(0), None)
    send_field(0, dot(mix_x[...], grid_columns(0)))
    field_back(0)
    image_0 = at_slots(0) + noise * start

    sums = sum_row(
        lane_sum(start * start),
        lane_sum(start * image_0),
        lane_sum(image_0 * image_0),
        lane_sum(noise * start * image_0),
        lane_sum(noise * image_0 * image_0),
    )
    own = totals_of(sums, 2)
    spread_out(1, image_0 - quotient(own[1], own[0]) * start, group_tile(sums))
    spread_plain(image_0)
    blocks = arrived_blocks(1)
    member_sums = group_rows(recv_a[1])
    group_sums = jnp.sum(member_sums, axis=0, keepdims=True)
    members = totals_of(member_sums, 2)
    group = totals_of(group_sums, 2)
    part = quotient(members[1], members[0]) - quotient(group[1], group[0])
    blocks = [
        blocks[place] + part[place : place + 1, :] * recv_a[0, place].astype(F32)
        for place in range(GROUP)
    ]
    mix_along_y(1, blocks, chip_tile(group_sums))
    fold_plain()
    grid_columns(1)
    chip_sums = chip_rows(recv_b[1])
    chips = totals_of(chip_sums, 2)
    rr, along, square, noise_01, noise_11 = totals_of(
        jnp.sum(chip_sums, axis=0, keepdims=True), 5
    )
    step_0 = rr / along
    grow = step_0 * (square / along)
    ratio = jnp.maximum(grow - 1.0, 0.0)
    new = rr * ratio
    part = grow - step_0 * quotient(chips[1], chips[0])
    columns = jnp.concatenate(
        [
            part[place : place + 1, :] * recv_b[0, place].astype(F32)
            - step_0 * recv_b[1, place].astype(F32)
            for place in range(CHIPS)
        ],
        axis=0,
    )
    field = dot(mix_x[...], columns.astype(BF16))
    send_field(1, field)
    inner = jnp.sum(jnp.sum(field * spread_columns(), axis=0, keepdims=True), axis=1, keepdims=True)
    inner = jnp.broadcast_to(inner, (8, 128))
    sums_sent[0] = inner
    sums_group[member] = inner
    copy_group(lambda place: sums_sent.at[0], sums_group, sum_sem.at[2], sum_sem.at[3])
    field_back(1)
    wait_bytes(sums_group, GROUP - 1, sum_sem.at[3])
    inner = jnp.sum(sums_group[...], axis=0)
    sums_sent[1] = inner
    sums_chips[chip] = inner
    copy_chips(lambda place: sums_sent.at[1], sums_chips, sum_sem.at[0], sum_sem.at[1])
    direction = grow * start - step_0 * image_0
    image_1 = at_slots(1) + noise * direction
    wait_bytes(sums_chips, CHIPS - 1, sum_sem.at[1])
    inner = jnp.sum(sums_chips[...], axis=0)[:1, :1]
    curvature = -step_0 * (inner + grow * noise_01 - step_0 * noise_11)
    step_1 = new / curvature
    solved = step_0 * start + step_1 * direction
    rest = start - step_0 * image_0 - step_1 * image_1
    for k in range(TILES):
        result_ref[0, 0, 0, k : k + 1, :] = solved[:, CAP * k : CAP * (k + 1)]
        result_ref[1, 0, 0, k : k + 1, :] = rest[:, CAP * k : CAP * (k + 1)]

    for turn_index in range(ITERS):
        wait_bytes(recv_a.at[turn_index], GROUP - 1, send_sem.at[turn_index, 0])
        wait_bytes(recv_b.at[turn_index], CHIPS - 1, send_sem.at[turn_index, 1])
        wait_bytes(recv_c.at[turn_index], CHIPS - 1, send_sem.at[turn_index, 2])
        wait_bytes(recv_d.at[turn_index], GROUP - 1, send_sem.at[turn_index, 3])
    wait_bytes(recv_ga, GROUP - 1, plain_sem.at[0])
    wait_bytes(recv_gb, CHIPS - 1, plain_sem.at[2])
    wait_bytes(sums_chips, CHIPS - 1, sum_sem.at[0])
    wait_bytes(sums_group, GROUP - 1, sum_sem.at[2])


def per_device(cells, offsets, counts, observed, noise, kernel_x, kernel_y, kernel_t):
    vmem = pl.BlockSpec(memory_space=pltpu.VMEM)
    whole = pl.BlockSpec(memory_space=pltpu.HBM)
    group_block = pltpu.VMEM((ITERS, GROUP, 32, 128), BF16)
    chip_block = pltpu.VMEM((ITERS, CHIPS, 16, 128), BF16)
    time_block = pltpu.VMEM((ITERS, 8, 4, 16, 128), BF16)
    operands = (cells, offsets, counts, observed, noise, kernel_x, kernel_y, kernel_t)
    result = pl.pallas_call(
        kernel,
        out_shape=jax.ShapeDtypeStruct((2, *observed.shape), F32),
        in_specs=[whole] * 8,
        out_specs=vmem,
        scratch_shapes=[pltpu.VMEM(operand.shape, operand.dtype) for operand in operands]
        + [
            pltpu.VMEM((NY, SLOTS), BF16),
            pltpu.VMEM((NT, SLOTS), F32),
            pltpu.VMEM((NT, SLOTS), F32),
            pltpu.VMEM((2 * NY, NY), BF16),
            pltpu.VMEM((NY, NY), BF16),
            pltpu.VMEM((NY, NY), BF16),
            pltpu.VMEM((4, NT + 16, 128), F32),
            group_block,
            group_block,
            time_block,
            chip_block,
            chip_block,
            chip_block,
            group_block,
            group_block,
            pltpu.VMEM((GROUP, 32, 128), BF16),
            pltpu.VMEM((GROUP, 32, 128), BF16),
            pltpu.VMEM((8, 4, 16, 128), BF16),
            pltpu.VMEM((CHIPS, 16, 128), BF16),
            pltpu.VMEM((2, 8, 128), F32),
            pltpu.VMEM((CHIPS, 8, 128), F32),
            pltpu.VMEM((GROUP, 8, 128), F32),
            pltpu.SemaphoreType.DMA((8,)),
            pltpu.SemaphoreType.DMA((ITERS, 4)),
            pltpu.SemaphoreType.DMA((ITERS, 4)),
            pltpu.SemaphoreType.DMA((4,)),
            pltpu.SemaphoreType.DMA((4,)),
            pltpu.SemaphoreType.REGULAR,
        ],
        compiler_params=pltpu.CompilerParams(
            collective_id=0, has_side_effects=True, vmem_limit_bytes=63 * 1024 * 1024
        ),
    )(*operands)
    return result[0], result[1]


def solution(mesh):
    placed = (
        P(None, "gx", "gy", None, None),
        P(None, "gx", "gy", None, None),
        P("gx", "gy", None),
        P("gx", "gy", None, None),
        P("gx", "gy", None, None),
        P(),
        P(),
        P(),
    )
    return jax.shard_map(
        per_device,
        mesh=mesh,
        in_specs=placed,
        out_specs=(P("gx", "gy", None, None), P("gx", "gy", None, None)),
        check_vma=False,
    )
```
